128 devices in a mesh: group: 4 (over x_hi, core), blk: 32 (over x_lo, z, y).
Axes of the slice: x: 4 (x_hi: 2, x_lo: 2; x = x_hi * 2 + x_lo), y: 4, z: 4, core: 2. Of those that a mesh axis runs over, the one named last changes fastest.
Arguments:
- image: float32 [16384, 1024], P(('group', 'blk')), may hold values from -8 to 8
- text: float32 [16384, 1024], P(('group', 'blk')), may hold values from -8 to 8
- pair: int32 [16384], P(('group', 'blk')), may hold values from 0 to 16383, as said below
Outputs:
- row_loss: float32 [16384], P(('group', 'blk'))
- grad_image: float32 [16384, 1024], P(('group', 'blk'))
- grad_text: float32 [16384, 1024], P(('group', 'blk'))
The draws below stay inside these ranges and needn't reach their ends.
Inputs may be any that keep to these rules, and one draw needn't show every extreme that they name: `pair`: row r of block b of group g pairs with text row r of block (b + k) mod 32 of the same group, with k drawn per row.
All inputs are finite; a program needn't handle non-finite values.
Results may differ from the reference program's by a relative error of at most 0.0077.
Values may be sent and summed in bfloat16 or wider, within the bound.
A program may use at most 128 MiB of HBM per device.

```python
import math
import jax
import jax.numpy as jnp
from jax import lax

D = 1024
ROWS = 128
N_GROUP = 4
N_BLK = 32


def base_fields(key):
    shape = (N_GROUP * N_BLK * ROWS, D)
    normal_field = jax.random.normal(jax.random.fold_in(key, 101), shape, jnp.float32)
    return normal_field


def pair_rows(key):
    total_rows = N_GROUP * N_BLK * ROWS
    offsets = jax.random.randint(jax.random.fold_in(key, 103), (total_rows,), 0, N_BLK)
    positions = jnp.arange(total_rows, dtype=jnp.int32)
    row_in_block = positions % ROWS
    block_index = positions // ROWS % N_BLK
    group_index = positions // (ROWS * N_BLK)
    return group_index * (N_BLK * ROWS) + (block_index + offsets) % N_BLK * ROWS + row_in_block


def draw_pair(key, part):
    return pair_rows(key).astype(jnp.int32)


def draw_text(key, part):
    normal_field = base_fields(key)
    values = jnp.clip(normal_field, -6.0, 6.0)
    return values.astype(jnp.float32)


def draw_image(key, part):
    normal_field = base_fields(key)
    key = jax.random.fold_in(key, 2)
    key_values = jax.random.fold_in(key, 0)
    shape = normal_field.shape
    values = jnp.clip(jax.random.normal(key_values, shape, jnp.float32), -6.0, 6.0)
    return values.astype(jnp.float32)


def setup_inputs(seed: int = 0) -> dict:
    keys = jax.random.split(jax.random.key(seed), 4)
    return {
        "image": draw_image(jax.random.fold_in(keys[3], 71), 0),
        "text": draw_text(jax.random.fold_in(keys[3], 71), 0),
        "pair": draw_pair(jax.random.fold_in(keys[3], 71), 0),
    }


score_gain = 2.5

def product(left, right, contract):
    return lax.dot_general(left.astype(jnp.float32), right.astype(jnp.float32), contract, precision=lax.Precision.HIGHEST, preferred_element_type=jnp.float32)

def reference(image, text, pair):
    groups = N_GROUP
    blocks = N_BLK
    window_rows = blocks * ROWS
    images_bf = image.astype(jnp.bfloat16)
    texts_bf = text.astype(jnp.bfloat16)
    scaling = score_gain / math.sqrt(D)
    contract_cols = (((1,), (1,)), ((), ()))
    contract_rows = (((0,), (0,)), ((), ()))
    contract_plain = (((1,), (0,)), ((), ()))

    def visit(accumulated, device_index):
        group_index = device_index // blocks
        prior_index = (group_index + groups - 1) % groups
        local_images = lax.dynamic_slice_in_dim(images_bf, device_index * ROWS, ROWS, 0)
        own_texts = lax.dynamic_slice_in_dim(texts_bf, group_index * window_rows, window_rows, 0)
        prior_texts = lax.dynamic_slice_in_dim(texts_bf, prior_index * window_rows, window_rows, 0)
        local_pair = lax.dynamic_slice_in_dim(pair, device_index * ROWS, ROWS, 0) - group_index * window_rows
        score_own = product(local_images, own_texts, contract_cols) * scaling
        score_prior = product(local_images, prior_texts, contract_cols) * scaling
        row_peak = jnp.maximum(lax.optimization_barrier(jnp.max(score_own, axis=1)), lax.optimization_barrier(jnp.max(score_prior, axis=1)))[:, None]
        row_total = lax.optimization_barrier(jnp.sum(jnp.exp(score_own - row_peak), axis=1)) + lax.optimization_barrier(jnp.sum(jnp.exp(score_prior - row_peak), axis=1))
        row_lse = row_peak[:, 0] + jnp.log(row_total)
        columns = lax.broadcasted_iota(jnp.int32, (ROWS, window_rows), 1)
        matches = columns == local_pair[:, None]
        positive = lax.optimization_barrier(jnp.sum(jnp.where(matches, score_own, 0.0), axis=1))
        losses = row_lse - positive
        weight_own = jnp.exp(score_own - row_lse[:, None]).astype(jnp.bfloat16)
        weight_prior = jnp.exp(score_prior - row_lse[:, None]).astype(jnp.bfloat16)
        selector = matches.astype(jnp.bfloat16)
        grads = product(weight_own, own_texts, contract_plain) + product(weight_prior, prior_texts, contract_plain) - product(selector, own_texts, contract_plain)
        own_part = product(weight_own, local_images, contract_rows) - product(selector, local_images, contract_rows)
        prior_part = product(weight_prior, local_images, contract_rows)
        current = lax.dynamic_slice_in_dim(accumulated, group_index * window_rows, window_rows, 0)
        accumulated = lax.dynamic_update_slice_in_dim(accumulated, current + own_part, group_index * window_rows, 0)
        current = lax.dynamic_slice_in_dim(accumulated, prior_index * window_rows, window_rows, 0)
        accumulated = lax.dynamic_update_slice_in_dim(accumulated, current + prior_part, prior_index * window_rows, 0)
        return (accumulated, (losses, grads))
    initial = jnp.zeros((groups * window_rows, D), jnp.float32)
    grad_text, outputs = lax.scan(visit, initial, jnp.arange(groups * blocks, dtype=jnp.int32))
    row_loss = outputs[0].reshape(-1)
    grad_image = outputs[1].reshape(-1, D)
    return (row_loss, grad_image, grad_text)
```

```python
import functools
import math

import jax
import jax.numpy as jnp
from jax import lax
from jax.experimental import pallas as pl
from jax.experimental.pallas import tpu as pltpu
from jax.sharding import PartitionSpec as P

MESH = pl.DeviceIdType.MESH
score_gain = 2.5
CA = 512
NT = (((1,), (1,)), ((), ()))
TN = (((0,), (0,)), ((), ()))
NN = (((1,), (0,)), ((), ()))

OFFSET = (0, 3, 1, 2)
PLACE = [[OFFSET.index((OFFSET[a] + OFFSET[i]) % 4) for i in range(4)] for a in range(4)]
SEEN = [OFFSET.index((4 - OFFSET[a]) % 4) for a in range(4)]


def kernel(
    image_ref, text_ref, pair_ref, loss_ref, gi_ref, gt_ref,
    img, txt, pairs, est, peak, stats, lse_ref, wt,
    gif, gib, gtf, gtb, rp, rx, ra1, ra2, ra3, rb1, rb2, rt1, rt2,
    send_sem, recv_sem,
):
    g = lax.axis_index("group")
    b = lax.axis_index("blk")
    x, z, y = b // 16, (b // 4) % 4, b % 4
    px = 1 - x
    zs = [(z + o) % 4 for o in OFFSET]
    ys = [(y + o) % 4 for o in OFFSET]
    xs = [x, px]

    def at(xx, zz, yy):
        return (g, xx * 16 + zz * 4 + yy)

    def mates():
        return [(zi, xi) for zi in range(4) for xi in range(2) if (zi, xi) != (0, 0)]

    to_px = at(px, z, y)
    to_zm, to_zp = at(x, zs[1], y), at(x, zs[2], y)
    to_ym, to_yp = at(x, z, ys[1]), at(x, z, ys[2])
    next_g, last_g = (g + 1) % 4, (g + 3) % 4
    flip = lambda even: jnp.where(even, px, x)
    to_next = (next_g, flip(next_g % 2 == 0) * 16 + z * 4 + y)
    to_last = (last_g, flip(g % 2 == 0) * 16 + z * 4 + y)

    barrier = pltpu.get_barrier_semaphore()
    peers = [at(xs[xi], zs[zi], y) for zi, xi in mates()] + [to_ym, to_yp, to_next, to_last]
    for peer in peers:
        pl.semaphore_signal(barrier, inc=1, device_id=peer, device_id_type=MESH)

    img[0:128, :] = image_ref[...].astype(jnp.bfloat16)
    txt[0:128, :] = text_ref[...].astype(jnp.bfloat16)
    pairs[:, 0:128] = pair_ref[...]

    pl.semaphore_wait(barrier, len(peers))

    names = {}
    started = []

    def copy(name, src, dst, to):
        k = names.setdefault(name, len(names))
        return pltpu.make_async_remote_copy(
            src_ref=src, dst_ref=dst, send_sem=send_sem.at[k], recv_sem=recv_sem.at[k],
            device_id=to, device_id_type=MESH,
        )

    def send(name, src, dst, to):
        c = copy(name, src, dst, to)
        c.start()
        started.append(c)

    def arrived(name, dst):
        copy(name, dst, dst, to_px).wait_recv()

    def A(zi, xi):
        return img.at[zi * 256 + xi * 128 : zi * 256 + xi * 128 + 128, 0:CA]

    def B(zi, xi, lo=0, hi=128):
        return img.at[zi * 256 + xi * 128 + lo : zi * 256 + xi * 128 + hi, CA:1024]

    def T(s, lo=0, hi=128):
        return txt.at[s * 128 + lo : s * 128 + hi, :]

    send("T0", T(0), T(1), to_yp)
    send("T1", T(0), T(2), to_ym)
    send("A0", A(0, 0), A(0, 1), to_px)
    send("B0", B(0, 0), B(1, 0), to_zp)
    send("B1", B(0, 0), B(2, 0), to_zm)
    send("P0", T(0), T(4), to_next)
    send("A1", A(0, 0), A(1, 0), to_zp)
    send("A2", A(0, 0), A(2, 0), to_zm)
    send("B2", B(0, 0), B(0, 1), to_px)

    def chunk(zi, xi):
        return slice(zi * 256 + xi * 128, zi * 256 + xi * 128 + 128)

    for zi, xi in mates():
        send(f"I{zi}{xi}", pairs.at[:, 0:128], pairs.at[:, chunk(SEEN[zi], xi)], at(xs[xi], zs[zi], y))

    arrived("A0", A(0, 1))
    send("A3", A(0, 1), A(1, 1), to_zp)
    send("A4", A(0, 1), A(2, 1), to_zm)
    arrived("B0", B(1, 0))
    send("B3", B(1, 0, 0, 64), B(3, 0, 0, 64), to_zp)
    send("B5", B(1, 0), B(1, 1), to_px)
    arrived("B1", B(2, 0))
    send("B4", B(2, 0, 64, 128), B(3, 0, 64, 128), to_zm)
    send("B6", B(2, 0), B(2, 1), to_px)
    arrived("T0", T(1))
    send("T2", T(1, 0, 64), T(3, 0, 64), to_yp)
    send("P1", T(1), T(5), to_next)
    arrived("T1", T(2))
    send("T3", T(2, 64, 128), T(3, 64, 128), to_ym)
    send("P2", T(2), T(6), to_next)
    arrived("A1", A(1, 0))
    send("A5", A(1, 0), A(3, 0), to_zp)
    arrived("B3", B(3, 0, 0, 64))
    arrived("B4", B(3, 0, 64, 128))
    send("B7", B(3, 0), B(3, 1), to_px)
    arrived("A4", A(2, 1))
    send("A6", A(2, 1), A(3, 1), to_zm)
    arrived("T2", T(3, 0, 64))
    arrived("T3", T(3, 64, 128))
    send("P3", T(3), T(7), to_next)
    for zi, xi in mates():
        arrived(f"I{SEEN[zi]}{xi}", pairs.at[:, chunk(zi, xi)])

    scaling = score_gain / math.sqrt(1024)
    bases = [(g * 32 + x * 16 + z * 4 + ys[s]) * 128 for s in range(4)]
    row = lax.broadcasted_iota(jnp.int32, (128, 256), 0)

    def score(slot):
        cols = slice(slot * 256, slot * 256 + 256)
        top = jnp.full((1, 256), -jnp.inf, jnp.float32)
        for t in range(4):
            st = lax.dot_general(
                txt[t * 256 : t * 256 + 256, :], img[cols, :], NT, preferred_element_type=jnp.float32
            ) * scaling
            est[t * 256 : t * 256 + 256, cols] = st
            top = jnp.maximum(top, jnp.max(st, axis=0, keepdims=True))
        total = jnp.zeros((1, 256), jnp.float32)
        positive = jnp.zeros((1, 256), jnp.float32)
        wanted = pairs[:, cols]
        for t in range(8):
            st = est[t * 128 : t * 128 + 128, cols]
            if t < 4:
                match = row == wanted - bases[t]
                positive += jnp.sum(jnp.where(match, st, 0.0), axis=0, keepdims=True)
            e = jnp.exp(st - top)
            est[t * 128 : t * 128 + 128, cols] = e
            total += jnp.sum(e, axis=0, keepdims=True)
        peak[:, cols] = top
        stats[0, 0:1, cols] = top + jnp.log(total)
        stats[0, 1:2, cols] = positive

    for k in range(4):
        arrived(f"P{k}", T(4 + k))
    arrived("B2", B(0, 1))
    score(0)
    arrived("A3", A(1, 1))
    arrived("B5", B(1, 1))
    score(1)
    arrived("A2", A(2, 0))
    arrived("B6", B(2, 1))
    score(2)
    arrived("A5", A(3, 0))
    arrived("A6", A(3, 1))
    arrived("B7", B(3, 1))
    score(3)

    for zi, xi in mates():
        send(f"S{zi}{xi}", stats.at[0], stats.at[SEEN[zi] * 2 + xi], at(xs[xi], zs[zi], y))
    for zi, xi in mates():
        arrived(f"S{SEEN[zi]}{xi}", stats.at[zi * 2 + xi])

    def pieces(zi, xi, r):
        out = [[None, None] for _ in range(4)]
        for i in range(4):
            for j in range(2):
                out[PLACE[zi][i]][j ^ xi] = stats[zi * 2 + xi, r : r + 1, chunk(i, j)]
        return jnp.concatenate([out[i][j] for i in range(4) for j in range(2)], axis=1)

    everyone = [(zi, xi) for zi in range(4) for xi in range(2)]
    parts = [pieces(zi, xi, 0) for zi, xi in everyone]
    top = functools.reduce(jnp.maximum, parts)
    lse = top + jnp.log(sum(jnp.exp(p - top) for p in parts))
    lse_ref[...] = lse
    positive = sum(pieces(zi, xi, 1)[:, 0:128] for zi, xi in everyone)
    loss_ref[...] = lse[:, 0:128] - positive

    def weights(slot):
        cols = slice(slot * 256, slot * 256 + 256)
        factor = jnp.exp(peak[:, cols] - lse_ref[:, cols])
        wanted = pairs[:, cols]
        for t in range(8):
            w = est[t * 128 : t * 128 + 128, cols] * factor
            if t < 4:
                w = jnp.where(row == wanted - bases[t], w - 1.0, w)
            wt[t * 128 : t * 128 + 128, cols] = w.astype(jnp.bfloat16)

    for slot in range(4):
        weights(slot)

    def grad_text(slot):
        return lax.dot_general(
            wt[slot * 128 : slot * 128 + 128, :], img[...], NN, preferred_element_type=jnp.float32
        )

    def prior(slot):
        rows = slice((4 + slot) * 128, (5 + slot) * 128)
        gtb[rows, :] = grad_text(4 + slot).astype(jnp.bfloat16)
        send(f"q{slot}", gtb.at[rows, :], rp.at[slot], to_last)

    def own(slot):
        gtf[slot * 128 : slot * 128 + 128, :] = grad_text(slot)

    def gi_rows(slot, xi):
        return slice(slot * 256 + xi * 128, slot * 256 + xi * 128 + 128)

    def grad_image(slot):
        rows = slice(slot * 256, slot * 256 + 256)
        v = lax.dot_general(wt[:, rows], txt[...], TN, preferred_element_type=jnp.float32)
        gif[rows, :] = v
        gib[gi_rows(slot, 1), CA:1024] = v[128:256, CA:1024].astype(jnp.bfloat16)
        send(f"b{slot}", gib.at[gi_rows(slot, 1), CA:1024], rx.at[slot], to_px)

    def send_a(name, slot, xi, dst, to, more=None):
        rows = gi_rows(slot, xi)
        v = gif[rows, 0:CA]
        for m in more or []:
            v = v + m.astype(jnp.float32)
        gib[rows, 0:CA] = v.astype(jnp.bfloat16)
        send(name, gib.at[rows, 0:CA], dst, to)

    prior(3)
    grad_image(3)
    send_a("a0", 3, 0, ra1.at[0], to_zp)
    send_a("a1", 3, 1, ra1.at[1], to_zm)
    prior(1)
    prior(2)
    grad_image(1)
    send_a("a2", 1, 0, ra2.at[1, 0], to_zm)
    grad_image(2)
    send_a("a3", 2, 1, ra2.at[0, 1], to_zp)

    def b_sum(slot, lo, hi, more=None):
        rows = slice(slot * 256 + lo, slot * 256 + hi)
        v = gif[rows, CA:1024] + rx[slot, lo:hi, :].astype(jnp.float32)
        if more is not None:
            v = v + more.astype(jnp.float32)
        return rows, v

    def b_put(slot, lo, hi, more=None):
        rows, v = b_sum(slot, lo, hi, more)
        gib[rows, CA:1024] = v.astype(jnp.bfloat16)
        return gib.at[rows, CA:1024]

    arrived("b3", rx.at[3])
    send("b4", b_put(3, 0, 64), rb1.at[0], to_zp)
    send("b5", b_put(3, 64, 128), rb1.at[1], to_zm)
    arrived("a0", ra1.at[0])
    send_a("a4", 2, 0, ra2.at[0, 0], to_zp, [ra1[0]])
    arrived("a1", ra1.at[1])
    send_a("a5", 1, 1, ra2.at[1, 1], to_zm, [ra1[1]])
    prior(0)
    grad_image(0)
    own(3)

    def t_put(slot, lo, hi, more=None):
        v = gtf[slot * 128 + lo : slot * 128 + hi, :] + rp[slot, lo:hi, :].astype(jnp.float32)
        if more is not None:
            v = v + more.astype(jnp.float32)
        rows = slice(slot * 128 + lo, slot * 128 + hi)
        gtb[rows, :] = v.astype(jnp.bfloat16)
        return gtb.at[rows, :]

    arrived("q3", rp.at[3])
    send("t0", t_put(3, 0, 64), rt1.at[0], to_yp)
    send("t1", t_put(3, 64, 128), rt1.at[1], to_ym)
    own(1)
    own(2)
    arrived("b1", rx.at[1])
    arrived("b5", rb1.at[1])
    b_put(1, 0, 64)
    b_put(1, 64, 128, rb1[1])
    send("b6", gib.at[gi_rows(1, 0), CA:1024], rb2.at[1], to_zm)
    arrived("b2", rx.at[2])
    arrived("b4", rb1.at[0])
    b_put(2, 0, 64, rb1[0])
    b_put(2, 64, 128)
    send("b7", gib.at[gi_rows(2, 0), CA:1024], rb2.at[0], to_zp)
    arrived("q1", rp.at[1])
    arrived("t1", rt1.at[1])
    t_put(1, 0, 64)
    t_put(1, 64, 128, rt1[1])
    send("t2", gtb.at[128:256, :], rt2.at[1], to_ym)
    arrived("q2", rp.at[2])
    arrived("t0", rt1.at[0])
    t_put(2, 0, 64, rt1[0])
    t_put(2, 64, 128)
    send("t3", gtb.at[256:384, :], rt2.at[0], to_yp)
    own(0)
    arrived("a3", ra2.at[0, 1])
    arrived("a5", ra2.at[1, 1])
    send_a("a6", 0, 1, ra3, to_px, [ra2[0, 1], ra2[1, 1]])

    arrived("q0", rp.at[0])
    arrived("t2", rt2.at[1])
    arrived("t3", rt2.at[0])
    gt_ref[...] = (
        gtf[0:128, :] + rp[0].astype(jnp.float32)
        + rt2[0].astype(jnp.float32) + rt2[1].astype(jnp.float32)
    )
    arrived("b0", rx.at[0])
    arrived("b6", rb2.at[1])
    arrived("b7", rb2.at[0])
    gi_ref[:, CA:1024] = (
        gif[0:128, CA:1024] + rx[0].astype(jnp.float32)
        + rb2[0].astype(jnp.float32) + rb2[1].astype(jnp.float32)
    )
    arrived("a2", ra2.at[1, 0])
    arrived("a4", ra2.at[0, 0])
    arrived("a6", ra3)
    gi_ref[:, 0:CA] = (
        gif[0:128, 0:CA] + ra2[0, 0].astype(jnp.float32)
        + ra2[1, 0].astype(jnp.float32) + ra3[...].astype(jnp.float32)
    )
    for c in started:
        c.wait_send()


def local(image, text, pair):
    bf16, f32 = jnp.bfloat16, jnp.float32
    vmem = pl.BlockSpec(memory_space=pltpu.VMEM)
    CB = 1024 - CA
    loss, grad_image, grad_text = pl.pallas_call(
        kernel,
        out_shape=(
            jax.ShapeDtypeStruct((1, 128), f32),
            jax.ShapeDtypeStruct((128, 1024), f32),
            jax.ShapeDtypeStruct((128, 1024), f32),
        ),
        in_specs=[vmem] * 3,
        out_specs=(vmem,) * 3,
        scratch_shapes=[
            pltpu.VMEM((1024, 1024), bf16),
            pltpu.VMEM((1024, 1024), bf16),
            pltpu.VMEM((1, 1024), jnp.int32),
            pltpu.VMEM((1024, 1024), f32),
            pltpu.VMEM((1, 1024), f32),
            pltpu.VMEM((8, 2, 1024), f32),
            pltpu.VMEM((1, 1024), f32),
            pltpu.VMEM((1024, 1024), bf16),
            pltpu.VMEM((1024, 1024), f32),
            pltpu.VMEM((1024, 1024), bf16),
            pltpu.VMEM((512, 1024), f32),
            pltpu.VMEM((1024, 1024), bf16),
            pltpu.VMEM((4, 128, 1024), bf16),
            pltpu.VMEM((4, 128, CB), bf16),
            pltpu.VMEM((2, 128, CA), bf16),
            pltpu.VMEM((2, 2, 128, CA), bf16),
            pltpu.VMEM((128, CA), bf16),
            pltpu.VMEM((2, 64, CB), bf16),
            pltpu.VMEM((2, 128, CB), bf16),
            pltpu.VMEM((2, 64, 1024), bf16),
            pltpu.VMEM((2, 128, 1024), bf16),
            pltpu.SemaphoreType.DMA((64,)),
            pltpu.SemaphoreType.DMA((64,)),
        ],
        compiler_params=pltpu.CompilerParams(
            collective_id=0, has_side_effects=True, vmem_limit_bytes=56 * 1024 * 1024
        ),
        cost_estimate=pl.CostEstimate(
            flops=6 * 1024**3, bytes_accessed=2 * 1024 * 1024, transcendentals=1024 * 1024
        ),
    )(image, text, pair.reshape(1, 128))
    return loss.reshape(128), grad_image, grad_text


def solution(mesh):
    in_specs = (P(("group", "blk"), None), P(("group", "blk"), None), P(("group", "blk")))
    out_specs = (P(("group", "blk")), P(("group", "blk"), None), P(("group", "blk"), None))
    return jax.shard_map(local, mesh=mesh, in_specs=in_specs, out_specs=out_specs, check_vma=False)
```

```python
import functools
import math

import jax
import jax.numpy as jnp
from jax import lax
from jax.experimental import pallas as pl
from jax.experimental.pallas import tpu as pltpu
from jax.sharding import PartitionSpec as P

MESH = pl.DeviceIdType.MESH
score_gain = 2.5
CA = 512
NT = (((1,), (1,)), ((), ()))
TN = (((0,), (0,)), ((), ()))
NN = (((1,), (0,)), ((), ()))

OFFSET = (0, 3, 1, 2)
PLACE = [[OFFSET.index((OFFSET[a] + OFFSET[i]) % 4) for i in range(4)] for a in range(4)]
SEEN = [OFFSET.index((4 - OFFSET[a]) % 4) for a in range(4)]


def kernel(
    image_ref, text_ref, pair_ref, loss_ref, gi_ref, gt_ref,
    img, txt, pairs, est, peak, stats, lse_ref, loss, wt,
    gif, gib, gtf, gtb, rp, rx, ra1, ra2, ra3, rb1, rb2, rt1, rt2,
    send_sem, recv_sem, local_sem,
):
    g = lax.axis_index("group")
    b = lax.axis_index("blk")
    x, z, y = b // 16, (b // 4) % 4, b % 4
    px = 1 - x
    zs = [(z + o) % 4 for o in OFFSET]
    ys = [(y + o) % 4 for o in OFFSET]
    xs = [x, px]

    def at(xx, zz, yy):
        return (g, xx * 16 + zz * 4 + yy)

    def mates():
        return [(zi, xi) for zi in range(4) for xi in range(2) if (zi, xi) != (0, 0)]

    to_px = at(px, z, y)
    to_zm, to_zp = at(x, zs[1], y), at(x, zs[2], y)
    to_ym, to_yp = at(x, z, ys[1]), at(x, z, ys[2])
    next_g, last_g = (g + 1) % 4, (g + 3) % 4
    flip = lambda even: jnp.where(even, px, x)
    to_next = (next_g, flip(next_g % 2 == 0) * 16 + z * 4 + y)
    to_last = (last_g, flip(g % 2 == 0) * 16 + z * 4 + y)

    barrier = pltpu.get_barrier_semaphore()
    peers = [at(xs[xi], zs[zi], y) for zi, xi in mates()] + [to_ym, to_yp, to_next, to_last]
    for peer in peers:
        pl.semaphore_signal(barrier, inc=1, device_id=peer, device_id_type=MESH)

    text_in = pltpu.make_async_copy(text_ref, gtf.at[0:128, :], local_sem.at[0])
    image_in = pltpu.make_async_copy(image_ref, gif.at[0:128, :], local_sem.at[1])
    text_in.start()
    image_in.start()
    pairs[:, 0:128] = pair_ref[...]
    text_in.wait()
    txt[0:128, :] = gtf[0:128, :].astype(jnp.bfloat16)
    image_in.wait()
    img[0:128, :] = gif[0:128, :].astype(jnp.bfloat16)

    pl.semaphore_wait(barrier, len(peers))

    names = {}
    started = []

    def copy(name, src, dst, to):
        k = names.setdefault(name, len(names))
        return pltpu.make_async_remote_copy(
            src_ref=src, dst_ref=dst, send_sem=send_sem.at[k], recv_sem=recv_sem.at[k],
            device_id=to, device_id_type=MESH,
        )

    def send(name, src, dst, to):
        c = copy(name, src, dst, to)
        c.start()
        started.append(c)

    def arrived(name, dst):
        copy(name, dst, dst, to_px).wait_recv()

    def A(zi, xi):
        return img.at[zi * 256 + xi * 128 : zi * 256 + xi * 128 + 128, 0:CA]

    def B(zi, xi, lo=0, hi=128):
        return img.at[zi * 256 + xi * 128 + lo : zi * 256 + xi * 128 + hi, CA:1024]

    def T(s, lo=0, hi=128):
        return txt.at[s * 128 + lo : s * 128 + hi, :]

    send("T0a", T(0, 0, 64), T(1, 0, 64), to_yp)
    send("T1b", T(0, 64, 128), T(2, 64, 128), to_ym)
    send("B0", B(0, 0), B(1, 0), to_zp)
    send("B1", B(0, 0), B(2, 0), to_zm)
    send("A0", A(0, 0), A(0, 1), to_px)
    send("P0", T(0), T(4), to_next)
    send("T0b", T(0, 64, 128), T(1, 64, 128), to_yp)
    send("T1a", T(0, 0, 64), T(2, 0, 64), to_ym)
    send("A1", A(0, 0), A(1, 0), to_zp)
    send("A2", A(0, 0), A(2, 0), to_zm)
    send("B2", B(0, 0), B(0, 1), to_px)

    def chunk(zi, xi):
        return slice(zi * 256 + xi * 128, zi * 256 + xi * 128 + 128)

    for zi, xi in mates():
        send(f"I{zi}{xi}", pairs.at[:, 0:128], pairs.at[:, chunk(SEEN[zi], xi)], at(xs[xi], zs[zi], y))

    scaling = score_gain / math.sqrt(1024)
    bases = [(g * 32 + x * 16 + z * 4 + ys[s]) * 128 for s in range(4)]
    row = lax.broadcasted_iota(jnp.int32, (128, 256), 0)

    def score(slot, t):
        cols = slice(slot * 256, slot * 256 + 256)
        st = lax.dot_general(
            txt[t * 256 : t * 256 + 256, :], img[cols, :], NT, preferred_element_type=jnp.float32
        ) * scaling
        est[t * 256 : t * 256 + 256, cols] = st
        top = jnp.max(st, axis=0, keepdims=True)
        peak[:, cols] = top if t == 0 else jnp.maximum(peak[:, cols], top)

    def local_stats(slot):
        cols = slice(slot * 256, slot * 256 + 256)
        top = peak[:, cols]
        total = jnp.zeros((1, 256), jnp.float32)
        positive = jnp.zeros((1, 256), jnp.float32)
        wanted = pairs[:, cols]
        for t in range(8):
            st = est[t * 128 : t * 128 + 128, cols]
            if t < 4:
                match = row == wanted - bases[t]
                positive += jnp.sum(jnp.where(match, st, 0.0), axis=0, keepdims=True)
            e = jnp.exp(st - top)
            est[t * 128 : t * 128 + 128, cols] = e
            total += jnp.sum(e, axis=0, keepdims=True)
        stats[0, 0:1, cols] = top + jnp.log(total)
        stats[0, 1:2, cols] = positive

    arrived("B0", B(1, 0))
    send("B3", B(1, 0, 0, 64), B(3, 0, 0, 64), to_zp)
    send("B5", B(1, 0), B(1, 1), to_px)
    arrived("B1", B(2, 0))
    send("B4", B(2, 0, 64, 128), B(3, 0, 64, 128), to_zm)
    send("B6", B(2, 0), B(2, 1), to_px)
    arrived("T0a", T(1, 0, 64))
    send("T2", T(1, 0, 64), T(3, 0, 64), to_yp)
    send("P1a", T(1, 0, 64), T(5, 0, 64), to_next)
    arrived("T1b", T(2, 64, 128))
    send("T3", T(2, 64, 128), T(3, 64, 128), to_ym)
    send("P2b", T(2, 64, 128), T(6, 64, 128), to_next)
    arrived("A0", A(0, 1))
    send("A3", A(0, 1), A(1, 1), to_zp)
    send("A4", A(0, 1), A(2, 1), to_zm)
    arrived("T0b", T(1, 64, 128))
    send("P1b", T(1, 64, 128), T(5, 64, 128), to_next)
    arrived("T1a", T(2, 0, 64))
    send("P2a", T(2, 0, 64), T(6, 0, 64), to_next)
    for zi, xi in mates():
        arrived(f"I{SEEN[zi]}{xi}", pairs.at[:, chunk(zi, xi)])
    arrived("A1", A(1, 0))
    send("A5", A(1, 0), A(3, 0), to_zp)
    arrived("B2", B(0, 1))
    score(0, 0)
    arrived("B3", B(3, 0, 0, 64))
    arrived("B4", B(3, 0, 64, 128))
    send("B7", B(3, 0), B(3, 1), to_px)
    arrived("T2", T(3, 0, 64))
    send("P3a", T(3, 0, 64), T(7, 0, 64), to_next)
    arrived("T3", T(3, 64, 128))
    send("P3b", T(3, 64, 128), T(7, 64, 128), to_next)
    score(0, 1)
    arrived("A4", A(2, 1))
    send("A6", A(2, 1), A(3, 1), to_zm)
    arrived("A3", A(1, 1))
    arrived("B5", B(1, 1))
    score(1, 0)
    score(1, 1)
    arrived("A2", A(2, 0))
    arrived("B6", B(2, 1))
    score(2, 0)
    score(2, 1)
    arrived("P0", T(4))
    arrived("P1a", T(5, 0, 64))
    arrived("P1b", T(5, 64, 128))
    for slot in range(3):
        score(slot, 2)
    arrived("P2a", T(6, 0, 64))
    arrived("P2b", T(6, 64, 128))
    arrived("P3a", T(7, 0, 64))
    arrived("P3b", T(7, 64, 128))
    for slot in range(3):
        score(slot, 3)
        local_stats(slot)
    arrived("A5", A(3, 0))
    arrived("A6", A(3, 1))
    arrived("B7", B(3, 1))
    for t in range(4):
        score(3, t)
    local_stats(3)

    for zi, xi in mates():
        send(f"S{zi}{xi}", stats.at[0], stats.at[SEEN[zi] * 2 + xi], at(xs[xi], zs[zi], y))
    for zi, xi in mates():
        arrived(f"S{SEEN[zi]}{xi}", stats.at[zi * 2 + xi])

    def pieces(zi, xi, r):
        out = [[None, None] for _ in range(4)]
        for i in range(4):
            for j in range(2):
                out[PLACE[zi][i]][j ^ xi] = stats[zi * 2 + xi, r : r + 1, chunk(i, j)]
        return jnp.concatenate([out[i][j] for i in range(4) for j in range(2)], axis=1)

    everyone = [(zi, xi) for zi in range(4) for xi in range(2)]
    parts = [pieces(zi, xi, 0) for zi, xi in everyone]
    top = functools.reduce(jnp.maximum, parts)
    lse = top + jnp.log(sum(jnp.exp(p - top) for p in parts))
    lse_ref[...] = lse
    positive = sum(pieces(zi, xi, 1)[:, 0:128] for zi, xi in everyone)
    loss[...] = lse[:, 0:128] - positive

    def weights(slot):
        cols = slice(slot * 256, slot * 256 + 256)
        factor = jnp.exp(peak[:, cols] - lse_ref[:, cols])
        wanted = pairs[:, cols]
        for t in range(8):
            w = est[t * 128 : t * 128 + 128, cols] * factor
            if t < 4:
                w = jnp.where(row == wanted - bases[t], w - 1.0, w)
            wt[t * 128 : t * 128 + 128, cols] = w.astype(jnp.bfloat16)

    for slot in range(4):
        weights(slot)

    def grad_text(slot):
        return lax.dot_general(
            wt[slot * 128 : slot * 128 + 128, :], img[...], NN, preferred_element_type=jnp.float32
        )

    def prior(slot):
        rows = slice((4 + slot) * 128, (5 + slot) * 128)
        gtb[rows, :] = grad_text(4 + slot).astype(jnp.bfloat16)
        send(f"q{slot}", gtb.at[rows, :], rp.at[slot], to_last)

    def own(slot):
        gtf[slot * 128 : slot * 128 + 128, :] = grad_text(slot)

    def gi_rows(slot, xi):
        return slice(slot * 256 + xi * 128, slot * 256 + xi * 128 + 128)

    def grad_image(slot):
        rows = slice(slot * 256, slot * 256 + 256)
        v = lax.dot_general(wt[:, rows], txt[...], TN, preferred_element_type=jnp.float32)
        gif[rows, :] = v
        gib[gi_rows(slot, 1), CA:1024] = v[128:256, CA:1024].astype(jnp.bfloat16)
        send(f"b{slot}", gib.at[gi_rows(slot, 1), CA:1024], rx.at[slot], to_px)

    def send_a(name, slot, xi, dst, to, more=None):
        rows = gi_rows(slot, xi)
        v = gif[rows, 0:CA]
        for m in more or []:
            v = v + m.astype(jnp.float32)
        gib[rows, 0:CA] = v.astype(jnp.bfloat16)
        send(name, gib.at[rows, 0:CA], dst, to)

    def b_sum(slot, lo, hi, more=None):
        rows = slice(slot * 256 + lo, slot * 256 + hi)
        v = gif[rows, CA:1024] + rx[slot, lo:hi, :].astype(jnp.float32)
        if more is not None:
            v = v + more.astype(jnp.float32)
        gib[rows, CA:1024] = v.astype(jnp.bfloat16)
        return gib.at[rows, CA:1024]

    def t_sum(slot, lo, hi, more=None):
        v = gtf[slot * 128 + lo : slot * 128 + hi, :] + rp[slot, lo:hi, :].astype(jnp.float32)
        if more is not None:
            v = v + more.astype(jnp.float32)
        rows = slice(slot * 128 + lo, slot * 128 + hi)
        gtb[rows, :] = v.astype(jnp.bfloat16)
        return gtb.at[rows, :]

    prior(3)
    grad_image(3)
    send_a("a1", 3, 1, ra1.at[1], to_zm)
    send_a("a0", 3, 0, ra1.at[0], to_zp)
    grad_image(2)
    send_a("a3", 2, 1, ra2.at[0, 1], to_zp)
    grad_image(1)
    prior(1)
    prior(2)
    arrived("b3", rx.at[3])
    send("b4", b_sum(3, 0, 64), rb1.at[0], to_zp)
    send("b5", b_sum(3, 64, 128), rb1.at[1], to_zm)
    arrived("a1", ra1.at[1])
    send_a("a5", 1, 1, ra2.at[1, 1], to_zm, [ra1[1]])
    arrived("a0", ra1.at[0])
    send_a("a4", 2, 0, ra2.at[0, 0], to_zp, [ra1[0]])
    send_a("a2", 1, 0, ra2.at[1, 0], to_zm)
    grad_image(0)
    prior(0)
    own(3)
    arrived("q3", rp.at[3])
    send("t0", t_sum(3, 0, 64), rt1.at[0], to_yp)
    send("t1", t_sum(3, 64, 128), rt1.at[1], to_ym)
    own(1)
    own(2)
    arrived("b2", rx.at[2])
    b_sum(2, 64, 128)
    arrived("b4", rb1.at[0])
    b_sum(2, 0, 64, rb1[0])
    send("b7", gib.at[gi_rows(2, 0), CA:1024], rb2.at[0], to_zp)
    arrived("b1", rx.at[1])
    b_sum(1, 0, 64)
    arrived("b5", rb1.at[1])
    b_sum(1, 64, 128, rb1[1])
    send("b6", gib.at[gi_rows(1, 0), CA:1024], rb2.at[1], to_zm)
    arrived("q1", rp.at[1])
    t_sum(1, 0, 64)
    arrived("t1", rt1.at[1])
    t_sum(1, 64, 128, rt1[1])
    send("t2", gtb.at[128:256, :], rt2.at[1], to_ym)
    own(0)
    arrived("a3", ra2.at[0, 1])
    arrived("a5", ra2.at[1, 1])
    send_a("a6", 0, 1, ra3, to_px, [ra2[0, 1], ra2[1, 1]])
    arrived("q2", rp.at[2])
    t_sum(2, 64, 128)
    arrived("t0", rt1.at[0])
    t_sum(2, 0, 64, rt1[0])
    send("t3", gtb.at[256:384, :], rt2.at[0], to_yp)

    loss_out = pltpu.make_async_copy(loss.at[0], loss_ref, local_sem.at[2])
    loss_out.start()
    arrived("b0", rx.at[0])
    arrived("b6", rb2.at[1])
    arrived("b7", rb2.at[0])
    gif[0:128, CA:1024] = (
        gif[0:128, CA:1024] + rx[0].astype(jnp.float32)
        + rb2[0].astype(jnp.float32) + rb2[1].astype(jnp.float32)
    )
    arrived("q0", rp.at[0])
    arrived("t2", rt2.at[1])
    arrived("t3", rt2.at[0])
    gtf[0:128, :] = (
        gtf[0:128, :] + rp[0].astype(jnp.float32)
        + rt2[0].astype(jnp.float32) + rt2[1].astype(jnp.float32)
    )
    text_out = pltpu.make_async_copy(gtf.at[0:128, :], gt_ref, local_sem.at[0])
    text_out.start()
    arrived("a2", ra2.at[1, 0])
    arrived("a4", ra2.at[0, 0])
    arrived("a6", ra3)
    gif[0:128, 0:CA] = (
        gif[0:128, 0:CA] + ra2[0, 0].astype(jnp.float32)
        + ra2[1, 0].astype(jnp.float32) + ra3[...].astype(jnp.float32)
    )
    image_out = pltpu.make_async_copy(gif.at[0:128, :], gi_ref, local_sem.at[1])
    image_out.start()
    for c in started:
        c.wait_send()
    loss_out.wait()
    text_out.wait()
    image_out.wait()


def local(image, text, pair):
    bf16, f32 = jnp.bfloat16, jnp.float32
    vmem = pl.BlockSpec(memory_space=pltpu.VMEM)
    hbm = pl.BlockSpec(memory_space=pltpu.HBM)
    anywhere = pl.BlockSpec(memory_space=pl.ANY)
    CB = 1024 - CA
    loss, grad_image, grad_text = pl.pallas_call(
        kernel,
        out_shape=(
            jax.ShapeDtypeStruct((128,), f32),
            jax.ShapeDtypeStruct((128, 1024), f32),
            jax.ShapeDtypeStruct((128, 1024), f32),
        ),
        in_specs=[hbm, hbm, vmem],
        out_specs=(anywhere,) * 3,
        scratch_shapes=[
            pltpu.VMEM((1024, 1024), bf16),
            pltpu.VMEM((1024, 1024), bf16),
            pltpu.VMEM((1, 1024), jnp.int32),
            pltpu.VMEM((1024, 1024), f32),
            pltpu.VMEM((1, 1024), f32),
            pltpu.VMEM((8, 2, 1024), f32),
            pltpu.VMEM((1, 1024), f32),
            pltpu.VMEM((1, 128), f32),
            pltpu.VMEM((1024, 1024), bf16),
            pltpu.VMEM((1024, 1024), f32),
            pltpu.VMEM((1024, 1024), bf16),
            pltpu.VMEM((512, 1024), f32),
            pltpu.VMEM((1024, 1024), bf16),
            pltpu.VMEM((4, 128, 1024), bf16),
            pltpu.VMEM((4, 128, CB), bf16),
            pltpu.VMEM((2, 128, CA), bf16),
            pltpu.VMEM((2, 2, 128, CA), bf16),
            pltpu.VMEM((128, CA), bf16),
            pltpu.VMEM((2, 64, CB), bf16),
            pltpu.VMEM((2, 128, CB), bf16),
            pltpu.VMEM((2, 64, 1024), bf16),
            pltpu.VMEM((2, 128, 1024), bf16),
            pltpu.SemaphoreType.DMA((72,)),
            pltpu.SemaphoreType.DMA((72,)),
            pltpu.SemaphoreType.DMA((3,)),
        ],
        compiler_params=pltpu.CompilerParams(
            collective_id=0, has_side_effects=True, vmem_limit_bytes=52 * 1024 * 1024 + 640 * 1024
        ),
        cost_estimate=pl.CostEstimate(
            flops=6 * 1024**3, bytes_accessed=2 * 1024 * 1024, transcendentals=1024 * 1024
        ),
    )(image, text, pair.reshape(1, 128))
    return loss, grad_image, grad_text


def solution(mesh):
    in_specs = (P(("group", "blk"), None), P(("group", "blk"), None), P(("group", "blk")))
    out_specs = (P(("group", "blk")), P(("group", "blk"), None), P(("group", "blk"), None))
    return jax.shard_map(local, mesh=mesh, in_specs=in_specs, out_specs=out_specs, check_vma=False)
```

```python
import functools
import math

import jax
import jax.numpy as jnp
from jax import lax
from jax.experimental import pallas as pl
from jax.experimental.pallas import tpu as pltpu
from jax.sharding import PartitionSpec as P

MESH = pl.DeviceIdType.MESH
score_gain = 2.5
CA = 512
NT = (((1,), (1,)), ((), ()))
TN = (((0,), (0,)), ((), ()))
NN = (((1,), (0,)), ((), ()))

OFFSET = (0, 3, 1, 2)
PLACE = [[OFFSET.index((OFFSET[a] + OFFSET[i]) % 4) for i in range(4)] for a in range(4)]
SEEN = [OFFSET.index((4 - OFFSET[a]) % 4) for a in range(4)]


def kernel(
    image_ref, text_ref, pair_ref, loss_ref, gi_ref, gt_ref,
    img, txt, pairs, est, peak, stats, wt,
    gif, gib, gtf, gtb, ru, rp, rx, ra1, ra2, ra3, rb1, rb2, rt1, rt2,
    send_sem, recv_sem, local_sem,
):
    g = lax.axis_index("group")
    b = lax.axis_index("blk")
    x, z, y = b // 16, (b // 4) % 4, b % 4
    px = 1 - x
    zs = [(z + o) % 4 for o in OFFSET]
    ys = [(y + o) % 4 for o in OFFSET]
    xs = [x, px]

    def at(xx, zz, yy):
        return (g, xx * 16 + zz * 4 + yy)

    def mates():
        return [(zi, xi) for zi in range(4) for xi in range(2) if (zi, xi) != (0, 0)]

    to_px = at(px, z, y)
    to_zm, to_zp = at(x, zs[1], y), at(x, zs[2], y)
    to_ym, to_yp = at(x, z, ys[1]), at(x, z, ys[2])
    next_g, last_g = (g + 1) % 4, (g + 3) % 4
    flip = lambda even: jnp.where(even, px, x)
    to_next = (next_g, flip(next_g % 2 == 0) * 16 + z * 4 + y)
    to_last = (last_g, flip(g % 2 == 0) * 16 + z * 4 + y)

    barrier = pltpu.get_barrier_semaphore()
    peers = [at(xs[xi], zs[zi], y) for zi, xi in mates()] + [to_ym, to_yp, to_next, to_last]
    for peer in peers:
        pl.semaphore_signal(barrier, inc=1, device_id=peer, device_id_type=MESH)

    text_in = pltpu.make_async_copy(text_ref, gtf.at[0:128, :], local_sem.at[0])
    image_in = pltpu.make_async_copy(image_ref, gif.at[0:128, :], local_sem.at[1])
    text_in.start()
    image_in.start()
    pairs[:, 0:128] = pair_ref[...]
    text_in.wait()
    txt[0:128, :] = gtf[0:128, :].astype(jnp.bfloat16)
    image_in.wait()
    img[0:128, :] = gif[0:128, :].astype(jnp.bfloat16)

    pl.semaphore_wait(barrier, len(peers))

    names = {}
    started = []

    def copy(name, src, dst, to):
        k = names.setdefault(name, len(names))
        return pltpu.make_async_remote_copy(
            src_ref=src, dst_ref=dst, send_sem=send_sem.at[k], recv_sem=recv_sem.at[k],
            device_id=to, device_id_type=MESH,
        )

    def send(name, src, dst, to):
        c = copy(name, src, dst, to)
        c.start()
        started.append(c)

    def arrived(name, dst):
        copy(name, dst, dst, to_px).wait_recv()

    def A(zi, xi):
        return img.at[zi * 256 + xi * 128 : zi * 256 + xi * 128 + 128, 0:CA]

    def B(zi, xi, lo=0, hi=128):
        return img.at[zi * 256 + xi * 128 + lo : zi * 256 + xi * 128 + hi, CA:1024]

    def T(s, lo=0, hi=128):
        return txt.at[s * 128 + lo : s * 128 + hi, :]

    send("T0a", T(0, 0, 64), T(1, 0, 64), to_yp)
    send("T1b", T(0, 64, 128), T(2, 64, 128), to_ym)
    send("B0", B(0, 0), B(1, 0), to_zp)
    send("B1", B(0, 0), B(2, 0), to_zm)
    send("A0", A(0, 0), A(0, 1), to_px)
    send("P0", T(0), T(4), to_next)
    send("T0b", T(0, 64, 128), T(1, 64, 128), to_yp)
    send("T1a", T(0, 0, 64), T(2, 0, 64), to_ym)
    send("A1", A(0, 0), A(1, 0), to_zp)
    send("A2", A(0, 0), A(2, 0), to_zm)
    send("B2", B(0, 0), B(0, 1), to_px)

    def chunk(zi, xi):
        return slice(zi * 256 + xi * 128, zi * 256 + xi * 128 + 128)

    for zi, xi in mates():
        send(f"I{zi}{xi}", pairs.at[:, 0:128], pairs.at[:, chunk(SEEN[zi], xi)], at(xs[xi], zs[zi], y))

    scaling = score_gain / math.sqrt(1024)
    bases = [(g * 32 + x * 16 + z * 4 + ys[s]) * 128 for s in range(4)]
    row = lax.broadcasted_iota(jnp.int32, (128, 256), 0)

    def score(slot, t):
        cols = slice(slot * 256, slot * 256 + 256)
        st = lax.dot_general(
            txt[t * 256 : t * 256 + 256, :], img[cols, :], NT, preferred_element_type=jnp.float32
        ) * scaling
        est[t * 256 : t * 256 + 256, cols] = st
        top = jnp.max(st, axis=0, keepdims=True)
        peak[:, cols] = top if t == 0 else jnp.maximum(peak[:, cols], top)

    def local_stats(slot):
        cols = slice(slot * 256, slot * 256 + 256)
        top = peak[:, cols]
        total = jnp.zeros((1, 256), jnp.float32)
        positive = jnp.zeros((1, 256), jnp.float32)
        wanted = pairs[:, cols]
        for t in range(8):
            st = est[t * 128 : t * 128 + 128, cols]
            if t < 4:
                match = row == wanted - bases[t]
                positive += jnp.sum(jnp.where(match, st, 0.0), axis=0, keepdims=True)
            e = jnp.exp(st - top)
            est[t * 128 : t * 128 + 128, cols] = e
            total += jnp.sum(e, axis=0, keepdims=True)
        stats[0, 0:1, cols] = top + jnp.log(total)
        stats[0, 1:2, cols] = positive

    arrived("B0", B(1, 0))
    send("B3", B(1, 0, 0, 64), B(3, 0, 0, 64), to_zp)
    send("B5", B(1, 0), B(1, 1), to_px)
    arrived("B1", B(2, 0))
    send("B4", B(2, 0, 64, 128), B(3, 0, 64, 128), to_zm)
    send("B6", B(2, 0), B(2, 1), to_px)
    arrived("T0a", T(1, 0, 64))
    send("T2", T(1, 0, 64), T(3, 0, 64), to_yp)
    send("P1a", T(1, 0, 64), T(5, 0, 64), to_next)
    arrived("T1b", T(2, 64, 128))
    send("T3", T(2, 64, 128), T(3, 64, 128), to_ym)
    send("P2b", T(2, 64, 128), T(6, 64, 128), to_next)
    arrived("A0", A(0, 1))
    send("A3", A(0, 1), A(1, 1), to_zp)
    send("A4", A(0, 1), A(2, 1), to_zm)
    arrived("T0b", T(1, 64, 128))
    send("P1b", T(1, 64, 128), T(5, 64, 128), to_next)
    arrived("T1a", T(2, 0, 64))
    send("P2a", T(2, 0, 64), T(6, 0, 64), to_next)
    for zi, xi in mates():
        arrived(f"I{SEEN[zi]}{xi}", pairs.at[:, chunk(zi, xi)])
    arrived("A1", A(1, 0))
    send("A5", A(1, 0), A(3, 0), to_zp)
    arrived("B2", B(0, 1))
    score(0, 0)
    arrived("B3", B(3, 0, 0, 64))
    arrived("B4", B(3, 0, 64, 128))
    send("B7", B(3, 0), B(3, 1), to_px)
    arrived("T2", T(3, 0, 64))
    send("P3a", T(3, 0, 64), T(7, 0, 64), to_next)
    arrived("T3", T(3, 64, 128))
    send("P3b", T(3, 64, 128), T(7, 64, 128), to_next)
    score(0, 1)
    arrived("A4", A(2, 1))
    send("A6", A(2, 1), A(3, 1), to_zm)
    arrived("A3", A(1, 1))
    arrived("B5", B(1, 1))
    score(1, 0)
    score(1, 1)
    arrived("A2", A(2, 0))
    arrived("B6", B(2, 1))
    score(2, 0)
    score(2, 1)
    arrived("P0", T(4))
    arrived("P1a", T(5, 0, 64))
    arrived("P1b", T(5, 64, 128))
    for slot in range(3):
        score(slot, 2)
    arrived("P2a", T(6, 0, 64))
    arrived("P2b", T(6, 64, 128))
    arrived("P3a", T(7, 0, 64))
    arrived("P3b", T(7, 64, 128))
    for slot in range(3):
        score(slot, 3)
        local_stats(slot)
    arrived("A5", A(3, 0))
    arrived("A6", A(3, 1))
    arrived("B7", B(3, 1))
    for t in range(4):
        score(3, t)
    local_stats(3)

    for zi, xi in mates():
        send(f"S{zi}{xi}", stats.at[0], stats.at[SEEN[zi] * 2 + xi], at(xs[xi], zs[zi], y))
    for zi, xi in mates():
        arrived(f"S{SEEN[zi]}{xi}", stats.at[zi * 2 + xi])

    def pieces(zi, xi, r):
        out = [[None, None] for _ in range(4)]
        for i in range(4):
            for j in range(2):
                out[PLACE[zi][i]][j ^ xi] = stats[zi * 2 + xi, r : r + 1, chunk(i, j)]
        return jnp.concatenate([out[i][j] for i in range(4) for j in range(2)], axis=1)

    everyone = [(zi, xi) for zi in range(4) for xi in range(2)]
    parts = [pieces(zi, xi, 0) for zi, xi in everyone]
    top = functools.reduce(jnp.maximum, parts)
    lse = top + jnp.log(sum(jnp.exp(p - top) for p in parts))
    positive = sum(pieces(zi, xi, 1)[:, 0:128] for zi, xi in everyone)
    loss_ref[...] = (lse[:, 0:128] - positive)[0]

    factor = jnp.exp(peak[...] - lse)

    def weights(t):
        rows = slice(t * 128, t * 128 + 128)
        for slot in range(4):
            cols = slice(slot * 256, slot * 256 + 256)
            w = est[rows, cols] * factor[:, cols]
            if t < 4:
                w = jnp.where(row == pairs[:, cols] - bases[t], w - 1.0, w)
            wt[rows, cols] = w.astype(jnp.bfloat16)

    def grad_text(slot, count=1):
        rows = slice(slot * 128, (slot + count) * 128)
        gtf[rows, :] = lax.dot_general(wt[rows, :], img[...], NN, preferred_element_type=jnp.float32)

    def put(slot, lo, more=()):
        rows = slice(slot * 128 + lo, slot * 128 + lo + 64)
        v = gtf[rows, :]
        for m in more:
            v = v + m.astype(jnp.float32)
        gtb[rows, :] = v.astype(jnp.bfloat16)
        return gtb.at[rows, :]

    def send_q(slot, lo, more=()):
        send(f"q{slot}{lo}", put(4 + slot, lo, more), rp.at[slot, lo : lo + 64, :], to_last)

    def send_t(slot, lo, more=()):
        end, to = (1, to_ym) if slot == 1 else (0, to_yp)
        more = [rp[slot, lo : lo + 64, :], *more]
        send(f"t{slot}{lo}", put(slot, lo, more), rt2.at[end, lo : lo + 64, :], to)

    def gi_rows(slot, xi, lo=0, hi=128):
        return slice(slot * 256 + xi * 128 + lo, slot * 256 + xi * 128 + hi)

    def grad_image(slot):
        rows = slice(slot * 256, slot * 256 + 256)
        v = lax.dot_general(wt[:, rows], txt[...], TN, preferred_element_type=jnp.float32)
        gif[rows, :] = v
        gib[gi_rows(slot, 1), CA:1024] = v[128:256, CA:1024].astype(jnp.bfloat16)

    def send_b(slot):
        send(f"b{slot}", gib.at[gi_rows(slot, 1), CA:1024], rx.at[slot], to_px)

    def send_a(name, slot, xi, dst, to, more=(), lo=0, hi=128):
        rows = gi_rows(slot, xi, lo, hi)
        v = gif[rows, 0:CA]
        for m in more:
            v = v + m.astype(jnp.float32)
        gib[rows, 0:CA] = v.astype(jnp.bfloat16)
        send(name, gib.at[rows, 0:CA], dst, to)

    def b_sum(slot, lo, hi, more=None):
        rows = slice(slot * 256 + lo, slot * 256 + hi)
        v = gif[rows, CA:1024] + rx[slot, lo:hi, :].astype(jnp.float32)
        if more is not None:
            v = v + more.astype(jnp.float32)
        gib[rows, CA:1024] = v.astype(jnp.bfloat16)
        return gib.at[rows, CA:1024]

    weights(7)
    grad_text(7)
    send("u0", put(7, 0), ru.at[0], to_yp)
    send("u1", put(7, 64), ru.at[1], to_ym)
    weights(5)
    weights(6)
    grad_text(5, 2)
    send_q(1, 0)
    send_q(2, 64)
    for t in range(5):
        weights(t)
    grad_image(3)
    send_a("a1", 3, 1, ra1.at[1], to_zm)
    send_a("a0", 3, 0, ra1.at[0], to_zp)
    send_b(3)
    grad_text(3, 2)
    send_q(0, 0)
    send("t0", put(3, 0), rt1.at[0], to_yp)
    send("t1", put(3, 64), rt1.at[1], to_ym)
    grad_image(2)
    send_b(2)
    send_a("a3", 2, 1, ra2.at[0, 1], to_zp)
    grad_image(1)
    send_a("a2", 1, 0, ra2.at[1, 0], to_zm)
    send_b(1)
    arrived("u1", ru.at[1])
    send_q(1, 64, [ru[1]])
    arrived("u0", ru.at[0])
    send_q(2, 0, [ru[0]])
    send_q(0, 64)
    grad_image(0)
    send_b(0)
    arrived("a1", ra1.at[1])
    for half in range(2):
        lo = half * 64
        send_a(
            f"a5{half}", 1, 1, ra2.at[1, 1, lo : lo + 64, :], to_zm, [ra1[1, lo : lo + 64, :]], lo, lo + 64
        )
        if half == 0:
            arrived("b3", rx.at[3])
            send("b5", b_sum(3, 64, 128), rb1.at[1], to_zm)
            send("b4", b_sum(3, 0, 64), rb1.at[0], to_zp)
    arrived("a0", ra1.at[0])
    send_a("a4", 2, 0, ra2.at[0, 0], to_zp, [ra1[0]])
    grad_text(1, 2)
    arrived("q10", rp.at[1, 0:64, :])
    send_t(1, 0)
    arrived("q264", rp.at[2, 64:128, :])
    send_t(2, 64)
    grad_text(0)
    arrived("b2", rx.at[2])
    b_sum(2, 64, 128)
    arrived("b4", rb1.at[0])
    b_sum(2, 0, 64, rb1[0])
    send("b7", gib.at[gi_rows(2, 0), CA:1024], rb2.at[0], to_zp)
    arrived("t1", rt1.at[1])
    arrived("q164", rp.at[1, 64:128, :])
    send_t(1, 64, [rt1[1]])
    arrived("a3", ra2.at[0, 1])
    arrived("a50", ra2.at[1, 1, 0:64, :])
    send_a("a60", 0, 1, ra3.at[0:64, :], to_px, [ra2[0, 1, 0:64, :], ra2[1, 1, 0:64, :]], 0, 64)
    arrived("t0", rt1.at[0])
    arrived("q20", rp.at[2, 0:64, :])
    send_t(2, 0, [rt1[0]])
    arrived("b1", rx.at[1])
    b_sum(1, 0, 64)
    arrived("b5", rb1.at[1])
    b_sum(1, 64, 128, rb1[1])
    send("b6", gib.at[gi_rows(1, 0), CA:1024], rb2.at[1], to_zm)
    arrived("a51", ra2.at[1, 1, 64:128, :])
    send_a("a61", 0, 1, ra3.at[64:128, :], to_px, [ra2[0, 1, 64:128, :], ra2[1, 1, 64:128, :]], 64, 128)

    for lo in (0, 64):
        arrived(f"q0{lo}", rp.at[0, lo : lo + 64, :])
        arrived(f"t1{lo}", rt2.at[1, lo : lo + 64, :])
        arrived(f"t2{lo}", rt2.at[0, lo : lo + 64, :])
    gt_ref[...] = (
        gtf[0:128, :] + rp[0].astype(jnp.float32)
        + rt2[0].astype(jnp.float32) + rt2[1].astype(jnp.float32)
    )
    arrived("b0", rx.at[0])
    arrived("b6", rb2.at[1])
    arrived("b7", rb2.at[0])
    gi_ref[:, CA:1024] = (
        gif[0:128, CA:1024] + rx[0].astype(jnp.float32)
        + rb2[0].astype(jnp.float32) + rb2[1].astype(jnp.float32)
    )
    arrived("a2", ra2.at[1, 0])
    arrived("a4", ra2.at[0, 0])
    arrived("a60", ra3.at[0:64, :])
    arrived("a61", ra3.at[64:128, :])
    gi_ref[:, 0:CA] = (
        gif[0:128, 0:CA] + ra2[0, 0].astype(jnp.float32)
        + ra2[1, 0].astype(jnp.float32) + ra3[...].astype(jnp.float32)
    )
    assert len(names) <= 96
    for c in started:
        c.wait_send()


def local(image, text, pair):
    bf16, f32 = jnp.bfloat16, jnp.float32
    vmem = pl.BlockSpec(memory_space=pltpu.VMEM)
    hbm = pl.BlockSpec(memory_space=pltpu.HBM)
    CB = 1024 - CA
    loss, grad_image, grad_text = pl.pallas_call(
        kernel,
        out_shape=(
            jax.ShapeDtypeStruct((128,), f32),
            jax.ShapeDtypeStruct((128, 1024), f32),
            jax.ShapeDtypeStruct((128, 1024), f32),
        ),
        in_specs=[hbm, hbm, vmem],
        out_specs=(vmem,) * 3,
        scratch_shapes=[
            pltpu.VMEM((1024, 1024), bf16),
            pltpu.VMEM((1024, 1024), bf16),
            pltpu.VMEM((1, 1024), jnp.int32),
            pltpu.VMEM((1024, 1024), f32),
            pltpu.VMEM((1, 1024), f32),
            pltpu.VMEM((8, 2, 1024), f32),
            pltpu.VMEM((1024, 1024), bf16),
            pltpu.VMEM((1024, 1024), f32),
            pltpu.VMEM((1024, 1024), bf16),
            pltpu.VMEM((1024, 1024), f32),
            pltpu.VMEM((1024, 1024), bf16),
            pltpu.VMEM((2, 64, 1024), bf16),
            pltpu.VMEM((3, 128, 1024), bf16),
            pltpu.VMEM((4, 128, CB), bf16),
            pltpu.VMEM((2, 128, CA), bf16),
            pltpu.VMEM((2, 2, 128, CA), bf16),
            pltpu.VMEM((128, CA), bf16),
            pltpu.VMEM((2, 64, CB), bf16),
            pltpu.VMEM((2, 128, CB), bf16),
            pltpu.VMEM((2, 64, 1024), bf16),
            pltpu.VMEM((2, 128, 1024), bf16),
            pltpu.SemaphoreType.DMA((96,)),
            pltpu.SemaphoreType.DMA((96,)),
            pltpu.SemaphoreType.DMA((2,)),
        ],
        compiler_params=pltpu.CompilerParams(
            collective_id=0, has_side_effects=True, vmem_limit_bytes=52 * 1024 * 1024 + 640 * 1024
        ),
        cost_estimate=pl.CostEstimate(
            flops=6 * 1024**3, bytes_accessed=2 * 1024 * 1024, transcendentals=1024 * 1024
        ),
    )(image, text, pair.reshape(1, 128))
    return loss, grad_image, grad_text


def solution(mesh):
    in_specs = (P(("group", "blk"), None), P(("group", "blk"), None), P(("group", "blk")))
    out_specs = (P(("group", "blk")), P(("group", "blk"), None), P(("group", "blk"), None))
    return jax.shard_map(local, mesh=mesh, in_specs=in_specs, out_specs=out_specs, check_vma=False)
```

```python
import functools
import math

import jax
import jax.numpy as jnp
from jax import lax
from jax.experimental import pallas as pl
from jax.experimental.pallas import tpu as pltpu
from jax.sharding import PartitionSpec as P

MESH = pl.DeviceIdType.MESH
score_gain = 2.5
CA = 512
NT = (((1,), (1,)), ((), ()))
TN = (((0,), (0,)), ((), ()))
NN = (((1,), (0,)), ((), ()))

OFFSET = (0, 3, 1, 2)
PLACE = [[OFFSET.index((OFFSET[a] + OFFSET[i]) % 4) for i in range(4)] for a in range(4)]
SEEN = [OFFSET.index((4 - OFFSET[a]) % 4) for a in range(4)]


def kernel(
    image_ref, text_ref, pair_ref, loss_ref, gi_ref, gt_ref, gi_last_ref, gt_last_ref,
    img, txt, pairs, est, peak, stats, wt,
    gif, gib, gtf, gtb, ru, rp, rx, ra1, ra2, ra3, rb1, rb2, rt1, rt2,
    send_sem, recv_sem, local_sem,
):
    g = lax.axis_index("group")
    b = lax.axis_index("blk")
    x, z, y = b // 16, (b // 4) % 4, b % 4
    px = 1 - x
    zs = [(z + o) % 4 for o in OFFSET]
    ys = [(y + o) % 4 for o in OFFSET]
    xs = [x, px]

    def at(xx, zz, yy):
        return (g, xx * 16 + zz * 4 + yy)

    def mates():
        return [(zi, xi) for zi in range(4) for xi in range(2) if (zi, xi) != (0, 0)]

    to_px = at(px, z, y)
    to_zm, to_zp = at(x, zs[1], y), at(x, zs[2], y)
    to_ym, to_yp = at(x, z, ys[1]), at(x, z, ys[2])
    next_g, last_g = (g + 1) % 4, (g + 3) % 4
    flip = lambda even: jnp.where(even, px, x)
    to_next = (next_g, flip(next_g % 2 == 0) * 16 + z * 4 + y)
    to_last = (last_g, flip(g % 2 == 0) * 16 + z * 4 + y)

    barrier = pltpu.get_barrier_semaphore()
    peers = [at(xs[xi], zs[zi], y) for zi, xi in mates()] + [to_ym, to_yp, to_next, to_last]
    for peer in peers:
        pl.semaphore_signal(barrier, inc=1, device_id=peer, device_id_type=MESH)

    text_in = pltpu.make_async_copy(text_ref, gtf.at[0:128, :], local_sem.at[0])
    image_in = pltpu.make_async_copy(image_ref, gif.at[0:128, :], local_sem.at[1])
    text_in.start()
    image_in.start()
    pairs[:, 0:128] = pair_ref[...]
    text_in.wait()
    txt[0:128, :] = gtf[0:128, :].astype(jnp.bfloat16)
    image_in.wait()
    img[0:128, :] = gif[0:128, :].astype(jnp.bfloat16)

    pl.semaphore_wait(barrier, len(peers))

    names = {}
    started = []

    def copy(name, src, dst, to):
        k = names.setdefault(name, len(names))
        return pltpu.make_async_remote_copy(
            src_ref=src, dst_ref=dst, send_sem=send_sem.at[k], recv_sem=recv_sem.at[k],
            device_id=to, device_id_type=MESH,
        )

    def send(name, src, dst, to):
        c = copy(name, src, dst, to)
        c.start()
        started.append(c)

    def arrived(name, dst):
        copy(name, dst, dst, to_px).wait_recv()

    def A(zi, xi, lo=0, hi=128):
        return img.at[zi * 256 + xi * 128 + lo : zi * 256 + xi * 128 + hi, 0:CA]

    def B(zi, xi, lo=0, hi=128):
        return img.at[zi * 256 + xi * 128 + lo : zi * 256 + xi * 128 + hi, CA:1024]

    def T(s, lo=0, hi=128):
        return txt.at[s * 128 + lo : s * 128 + hi, :]

    send("T0a", T(0, 0, 64), T(1, 0, 64), to_yp)
    send("T1b", T(0, 64, 128), T(2, 64, 128), to_ym)
    send("B0", B(0, 0), B(1, 0), to_zp)
    send("B1", B(0, 0), B(2, 0), to_zm)
    send("A0", A(0, 0), A(0, 1), to_px)
    send("P0", T(0), T(4), to_next)
    def chunk(zi, xi):
        return slice(zi * 256 + xi * 128, zi * 256 + xi * 128 + 128)

    for zi, xi in mates():
        send(f"I{zi}{xi}", pairs.at[:, 0:128], pairs.at[:, chunk(SEEN[zi], xi)], at(xs[xi], zs[zi], y))
    send("T0b", T(0, 64, 128), T(1, 64, 128), to_yp)
    send("T1a", T(0, 0, 64), T(2, 0, 64), to_ym)
    send("A1", A(0, 0), A(1, 0), to_zp)
    send("A2", A(0, 0), A(2, 0), to_zm)
    send("B2", B(0, 0), B(0, 1), to_px)

    scaling = score_gain / math.sqrt(1024)
    bases = [(g * 32 + x * 16 + z * 4 + ys[s]) * 128 for s in range(4)]
    row = lax.broadcasted_iota(jnp.int32, (128, 256), 0)

    def score(slot, t):
        cols = slice(slot * 256, slot * 256 + 256)
        st = lax.dot_general(
            txt[t * 256 : t * 256 + 256, :], img[cols, :], NT, preferred_element_type=jnp.float32
        ) * scaling
        est[t * 256 : t * 256 + 256, cols] = st
        top = jnp.max(st, axis=0, keepdims=True)
        peak[:, cols] = top if t == 0 else jnp.maximum(peak[:, cols], top)

    def local_stats(slot):
        cols = slice(slot * 256, slot * 256 + 256)
        top = peak[:, cols]
        total = jnp.zeros((1, 256), jnp.float32)
        positive = jnp.zeros((1, 256), jnp.float32)
        wanted = pairs[:, cols]
        for t in range(8):
            st = est[t * 128 : t * 128 + 128, cols]
            if t < 4:
                match = row == wanted - bases[t]
                positive += jnp.sum(jnp.where(match, st, 0.0), axis=0, keepdims=True)
            e = jnp.exp(st - top)
            est[t * 128 : t * 128 + 128, cols] = e
            total += jnp.sum(e, axis=0, keepdims=True)
        stats[0, 0:1, cols] = top + jnp.log(total)
        stats[0, 1:2, cols] = positive

    arrived("B0", B(1, 0))
    send("B3", B(1, 0, 0, 64), B(3, 0, 0, 64), to_zp)
    send("B5", B(1, 0), B(1, 1), to_px)
    arrived("A0", A(0, 1))
    send("A40", A(0, 1, 0, 64), A(2, 1, 0, 64), to_zm)
    arrived("B1", B(2, 0))
    send("B4", B(2, 0, 64, 128), B(3, 0, 64, 128), to_zm)
    send("B6", B(2, 0), B(2, 1), to_px)
    send("A41", A(0, 1, 64, 128), A(2, 1, 64, 128), to_zm)
    arrived("T0a", T(1, 0, 64))
    send("P1a", T(1, 0, 64), T(5, 0, 64), to_next)
    send("T2", T(1, 0, 64), T(3, 0, 64), to_yp)
    arrived("T1b", T(2, 64, 128))
    send("P2b", T(2, 64, 128), T(6, 64, 128), to_next)
    send("T3", T(2, 64, 128), T(3, 64, 128), to_ym)
    send("A3", A(0, 1), A(1, 1), to_zp)
    arrived("T0b", T(1, 64, 128))
    send("P1b", T(1, 64, 128), T(5, 64, 128), to_next)
    arrived("T1a", T(2, 0, 64))
    send("P2a", T(2, 0, 64), T(6, 0, 64), to_next)
    arrived("A1", A(1, 0))
    send("A5", A(1, 0), A(3, 0), to_zp)
    arrived("B2", B(0, 1))
    arrived("A40", A(2, 1, 0, 64))
    send("A60", A(2, 1, 0, 64), A(3, 1, 0, 64), to_zm)
    arrived("P1a", T(5, 0, 64))
    send("U0", T(5, 0, 64), T(7, 0, 64), to_yp)
    arrived("P2b", T(6, 64, 128))
    send("U1", T(6, 64, 128), T(7, 64, 128), to_ym)
    arrived("B3", B(3, 0, 0, 64))
    arrived("B4", B(3, 0, 64, 128))
    send("B7", B(3, 0), B(3, 1), to_px)
    arrived("A41", A(2, 1, 64, 128))
    send("A61", A(2, 1, 64, 128), A(3, 1, 64, 128), to_zm)
    arrived("T2", T(3, 0, 64))
    arrived("T3", T(3, 64, 128))
    score(0, 0)
    score(0, 1)
    arrived("A3", A(1, 1))
    arrived("B5", B(1, 1))
    score(1, 0)
    score(1, 1)
    arrived("A2", A(2, 0))
    arrived("B6", B(2, 1))
    score(2, 0)
    score(2, 1)
    arrived("P0", T(4))
    arrived("P1b", T(5, 64, 128))
    score(0, 2)
    score(1, 2)
    score(2, 2)
    arrived("P2a", T(6, 0, 64))
    arrived("U0", T(7, 0, 64))
    arrived("U1", T(7, 64, 128))
    score(0, 3)
    score(1, 3)
    score(2, 3)
    for zi, xi in mates():
        arrived(f"I{SEEN[zi]}{xi}", pairs.at[:, chunk(zi, xi)])
    local_stats(0)
    local_stats(1)
    local_stats(2)
    arrived("A5", A(3, 0))
    arrived("A60", A(3, 1, 0, 64))
    arrived("A61", A(3, 1, 64, 128))
    arrived("B7", B(3, 1))
    for t in range(4):
        score(3, t)
    local_stats(3)

    for zi, xi in mates():
        send(f"S{zi}{xi}", stats.at[0], stats.at[SEEN[zi] * 2 + xi], at(xs[xi], zs[zi], y))
    for zi, xi in mates():
        arrived(f"S{SEEN[zi]}{xi}", stats.at[zi * 2 + xi])

    def pieces(zi, xi, r):
        out = [[None, None] for _ in range(4)]
        for i in range(4):
            for j in range(2):
                out[PLACE[zi][i]][j ^ xi] = stats[zi * 2 + xi, r : r + 1, chunk(i, j)]
        return jnp.concatenate([out[i][j] for i in range(4) for j in range(2)], axis=1)

    everyone = [(zi, xi) for zi in range(4) for xi in range(2)]
    parts = [pieces(zi, xi, 0) for zi, xi in everyone]
    top = functools.reduce(jnp.maximum, parts)
    lse = top + jnp.log(sum(jnp.exp(p - top) for p in parts))
    positive = sum(pieces(zi, xi, 1)[:, 0:128] for zi, xi in everyone)
    loss_ref[...] = (lse[:, 0:128] - positive)[0]

    factor = jnp.exp(peak[...] - lse)

    def weights(t):
        rows = slice(t * 128, t * 128 + 128)
        for slot in range(4):
            cols = slice(slot * 256, slot * 256 + 256)
            w = est[rows, cols] * factor[:, cols]
            if t < 4:
                w = jnp.where(row == pairs[:, cols] - bases[t], w - 1.0, w)
            wt[rows, cols] = w.astype(jnp.bfloat16)

    def grad_text(slot, count=1):
        rows = slice(slot * 128, (slot + count) * 128)
        gtf[rows, :] = lax.dot_general(wt[rows, :], img[...], NN, preferred_element_type=jnp.float32)

    def put(slot, lo, more=()):
        rows = slice(slot * 128 + lo, slot * 128 + lo + 64)
        v = gtf[rows, :]
        for m in more:
            v = v + m.astype(jnp.float32)
        gtb[rows, :] = v.astype(jnp.bfloat16)
        return gtb.at[rows, :]

    def send_q(slot, lo, more=()):
        send(f"q{slot}{lo}", put(4 + slot, lo, more), rp.at[slot, lo : lo + 64, :], to_last)

    def send_t(slot, lo, more=()):
        end, to = (1, to_ym) if slot == 1 else (0, to_yp)
        more = [rp[slot, lo : lo + 64, :], *more]
        send(f"t{slot}{lo}", put(slot, lo, more), rt2.at[end, lo : lo + 64, :], to)

    def gi_rows(slot, xi, lo=0, hi=128):
        return slice(slot * 256 + xi * 128 + lo, slot * 256 + xi * 128 + hi)

    def grad_image(slot):
        rows = slice(slot * 256, slot * 256 + 256)
        v = lax.dot_general(wt[:, rows], txt[...], TN, preferred_element_type=jnp.float32)
        gif[rows, :] = v
        gib[gi_rows(slot, 1), CA:1024] = v[128:256, CA:1024].astype(jnp.bfloat16)

    def send_b(slot):
        send(f"b{slot}", gib.at[gi_rows(slot, 1), CA:1024], rx.at[slot], to_px)

    def send_a(name, slot, xi, dst, to, more=(), lo=0, hi=128):
        rows = gi_rows(slot, xi, lo, hi)
        v = gif[rows, 0:CA]
        for m in more:
            v = v + m.astype(jnp.float32)
        gib[rows, 0:CA] = v.astype(jnp.bfloat16)
        send(name, gib.at[rows, 0:CA], dst, to)

    def b_sum(slot, lo, hi, more=None):
        rows = slice(slot * 256 + lo, slot * 256 + hi)
        v = gif[rows, CA:1024] + rx[slot, lo:hi, :].astype(jnp.float32)
        if more is not None:
            v = v + more.astype(jnp.float32)
        gib[rows, CA:1024] = v.astype(jnp.bfloat16)
        return gib.at[rows, CA:1024]

    weights(7)
    grad_text(7)
    send("u0", put(7, 0), ru.at[0], to_yp)
    send("u1", put(7, 64), ru.at[1], to_ym)
    weights(5)
    weights(6)
    grad_text(5, 2)
    send_q(1, 0)
    send_q(2, 64)
    for t in range(5):
        weights(t)
    grad_image(3)
    send_a("a1", 3, 1, ra1.at[1], to_zm)
    send_a("a0", 3, 0, ra1.at[0], to_zp)
    send_b(3)
    grad_text(3, 2)
    send_q(0, 0)
    send("t0", put(3, 0), rt1.at[0], to_yp)
    send("t1", put(3, 64), rt1.at[1], to_ym)
    grad_image(2)
    send_b(2)
    send_a("a3", 2, 1, ra2.at[0, 1], to_zp)
    grad_image(1)
    send_a("a2", 1, 0, ra2.at[1, 0], to_zm)
    send_b(1)
    arrived("u1", ru.at[1])
    send_q(1, 64, [ru[1]])
    arrived("u0", ru.at[0])
    send_q(2, 0, [ru[0]])
    send_q(0, 64)
    grad_image(0)
    send_b(0)
    arrived("a1", ra1.at[1])
    for half in range(2):
        lo = half * 64
        send_a(
            f"a5{half}", 1, 1, ra2.at[1, 1, lo : lo + 64, :], to_zm, [ra1[1, lo : lo + 64, :]], lo, lo + 64
        )
        if half == 0:
            arrived("b3", rx.at[3])
            send("b5", b_sum(3, 64, 128), rb1.at[1], to_zm)
            send("b4", b_sum(3, 0, 64), rb1.at[0], to_zp)
    arrived("a0", ra1.at[0])
    send_a("a4", 2, 0, ra2.at[0, 0], to_zp, [ra1[0]])
    grad_text(1, 2)
    arrived("q10", rp.at[1, 0:64, :])
    send_t(1, 0)
    arrived("q264", rp.at[2, 64:128, :])
    send_t(2, 64)
    grad_text(0)
    arrived("t1", rt1.at[1])
    arrived("q164", rp.at[1, 64:128, :])
    send_t(1, 64, [rt1[1]])
    arrived("b2", rx.at[2])
    b_sum(2, 64, 128)
    arrived("t0", rt1.at[0])
    arrived("q20", rp.at[2, 0:64, :])
    send_t(2, 0, [rt1[0]])
    arrived("a3", ra2.at[0, 1])
    arrived("a50", ra2.at[1, 1, 0:64, :])
    send_a("a60", 0, 1, ra3.at[0:64, :], to_px, [ra2[0, 1, 0:64, :], ra2[1, 1, 0:64, :]], 0, 64)
    arrived("b4", rb1.at[0])
    b_sum(2, 0, 64, rb1[0])
    send("b7", gib.at[gi_rows(2, 0), CA:1024], rb2.at[0], to_zp)
    arrived("b1", rx.at[1])
    b_sum(1, 0, 64)
    arrived("b5", rb1.at[1])
    b_sum(1, 64, 128, rb1[1])
    send("b6", gib.at[gi_rows(1, 0), CA:1024], rb2.at[1], to_zm)
    arrived("a51", ra2.at[1, 1, 64:128, :])
    send_a("a61", 0, 1, ra3.at[64:128, :], to_px, [ra2[0, 1, 64:128, :], ra2[1, 1, 64:128, :]], 64, 128)

    for lo in (0, 64):
        arrived(f"q0{lo}", rp.at[0, lo : lo + 64, :])
        arrived(f"t1{lo}", rt2.at[1, lo : lo + 64, :])
        arrived(f"t2{lo}", rt2.at[0, lo : lo + 64, :])
    gt_ref[...] = (
        gtf[0:128, :] + rp[0].astype(jnp.float32) + rt2[0].astype(jnp.float32)
    )
    gt_last_ref[...] = rt2[1]
    arrived("b0", rx.at[0])
    arrived("b6", rb2.at[1])
    arrived("b7", rb2.at[0])
    gi_ref[:, CA:1024] = (
        gif[0:128, CA:1024] + rx[0].astype(jnp.float32) + rb2[0].astype(jnp.float32)
    )
    gi_last_ref[:, CA:1024] = rb2[1]
    arrived("a2", ra2.at[1, 0])
    arrived("a4", ra2.at[0, 0])
    arrived("a60", ra3.at[0:64, :])
    arrived("a61", ra3.at[64:128, :])
    gi_ref[:, 0:CA] = (
        gif[0:128, 0:CA] + ra2[0, 0].astype(jnp.float32) + ra2[1, 0].astype(jnp.float32)
    )
    gi_last_ref[:, 0:CA] = ra3[...]
    assert len(names) <= 96
    for c in started:
        c.wait_send()


def local(image, text, pair):
    bf16, f32 = jnp.bfloat16, jnp.float32
    vmem = pl.BlockSpec(memory_space=pltpu.VMEM)
    hbm = pl.BlockSpec(memory_space=pltpu.HBM)
    CB = 1024 - CA
    loss, grad_image, grad_text, image_last, text_last = pl.pallas_call(
        kernel,
        out_shape=(
            jax.ShapeDtypeStruct((128,), f32),
            jax.ShapeDtypeStruct((128, 1024), f32),
            jax.ShapeDtypeStruct((128, 1024), f32),
            jax.ShapeDtypeStruct((128, 1024), bf16),
            jax.ShapeDtypeStruct((128, 1024), bf16),
        ),
        in_specs=[hbm, hbm, vmem],
        out_specs=(vmem,) * 5,
        scratch_shapes=[
            pltpu.VMEM((1024, 1024), bf16),
            pltpu.VMEM((1024, 1024), bf16),
            pltpu.VMEM((1, 1024), jnp.int32),
            pltpu.VMEM((1024, 1024), f32),
            pltpu.VMEM((1, 1024), f32),
            pltpu.VMEM((8, 2, 1024), f32),
            pltpu.VMEM((1024, 1024), bf16),
            pltpu.VMEM((1024, 1024), f32),
            pltpu.VMEM((1024, 1024), bf16),
            pltpu.VMEM((1024, 1024), f32),
            pltpu.VMEM((1024, 1024), bf16),
            pltpu.VMEM((2, 64, 1024), bf16),
            pltpu.VMEM((3, 128, 1024), bf16),
            pltpu.VMEM((4, 128, CB), bf16),
            pltpu.VMEM((2, 128, CA), bf16),
            pltpu.VMEM((2, 2, 128, CA), bf16),
            pltpu.VMEM((128, CA), bf16),
            pltpu.VMEM((2, 64, CB), bf16),
            pltpu.VMEM((2, 128, CB), bf16),
            pltpu.VMEM((2, 64, 1024), bf16),
            pltpu.VMEM((2, 128, 1024), bf16),
            pltpu.SemaphoreType.DMA((96,)),
            pltpu.SemaphoreType.DMA((96,)),
            pltpu.SemaphoreType.DMA((2,)),
        ],
        compiler_params=pltpu.CompilerParams(
            collective_id=0, has_side_effects=True, vmem_limit_bytes=52 * 1024 * 1024 + 128 * 1024
        ),
        cost_estimate=pl.CostEstimate(
            flops=6 * 1024**3, bytes_accessed=2 * 1024 * 1024, transcendentals=1024 * 1024
        ),
    )(image, text, pair.reshape(1, 128))
    return loss, grad_image + image_last.astype(f32), grad_text + text_last.astype(f32)


def solution(mesh):
    in_specs = (P(("group", "blk"), None), P(("group", "blk"), None), P(("group", "blk")))
    out_specs = (P(("group", "blk")), P(("group", "blk"), None), P(("group", "blk"), None))
    return jax.shard_map(local, mesh=mesh, in_specs=in_specs, out_specs=out_specs, check_vma=False)
```

```python
import functools
import math

import jax
import jax.numpy as jnp
from jax import lax
from jax.experimental import pallas as pl
from jax.experimental.pallas import tpu as pltpu
from jax.sharding import PartitionSpec as P

MESH = pl.DeviceIdType.MESH
score_gain = 2.5
CA = 512
NT = (((1,), (1,)), ((), ()))
TN = (((0,), (0,)), ((), ()))
NN = (((1,), (0,)), ((), ()))

OFFSET = (0, 3, 1, 2)
PLACE = [[OFFSET.index((OFFSET[a] + OFFSET[i]) % 4) for i in range(4)] for a in range(4)]
SEEN = [OFFSET.index((4 - OFFSET[a]) % 4) for a in range(4)]


def kernel(
    image_ref, text_ref, pair_ref, loss_ref, gi_ref, gt_ref, gi_last_ref, gt_last_ref,
    img, txt, pairs, est, peak, stats, wt,
    ebf, chosen, across, gis, gif, gib, gtf, gtb, ru, rp, rx, ra1, ra2, ra3, rb1, rb2, rt1, rt2,
    send_sem, recv_sem, local_sem,
):
    g = lax.axis_index("group")
    b = lax.axis_index("blk")
    x, z, y = b // 16, (b // 4) % 4, b % 4
    px = 1 - x
    zs = [(z + o) % 4 for o in OFFSET]
    ys = [(y + o) % 4 for o in OFFSET]
    xs = [x, px]

    def at(xx, zz, yy):
        return (g, xx * 16 + zz * 4 + yy)

    def mates():
        return [(zi, xi) for zi in range(4) for xi in range(2) if (zi, xi) != (0, 0)]

    to_px = at(px, z, y)
    to_zm, to_zp = at(x, zs[1], y), at(x, zs[2], y)
    to_ym, to_yp = at(x, z, ys[1]), at(x, z, ys[2])
    next_g, last_g = (g + 1) % 4, (g + 3) % 4
    flip = lambda even: jnp.where(even, px, x)
    to_next = (next_g, flip(next_g % 2 == 0) * 16 + z * 4 + y)
    to_last = (last_g, flip(g % 2 == 0) * 16 + z * 4 + y)

    barrier = pltpu.get_barrier_semaphore()
    peers = [at(xs[xi], zs[zi], y) for zi, xi in mates()] + [to_ym, to_yp, to_next, to_last]
    for peer in peers:
        pl.semaphore_signal(barrier, inc=1, device_id=peer, device_id_type=MESH)

    text_in = pltpu.make_async_copy(text_ref, gtf.at[0:128, :], local_sem.at[0])
    image_in = pltpu.make_async_copy(image_ref, gif.at[0:128, :], local_sem.at[1])
    text_in.start()
    image_in.start()
    pairs[:, 0:128] = pair_ref[...]
    text_in.wait()
    txt[0:128, :] = gtf[0:128, :].astype(jnp.bfloat16)
    image_in.wait()
    img[0:128, :] = gif[0:128, :].astype(jnp.bfloat16)

    pl.semaphore_wait(barrier, len(peers))

    names = {}
    started = []

    def copy(name, src, dst, to):
        k = names.setdefault(name, len(names))
        return pltpu.make_async_remote_copy(
            src_ref=src, dst_ref=dst, send_sem=send_sem.at[k], recv_sem=recv_sem.at[k],
            device_id=to, device_id_type=MESH,
        )

    def send(name, src, dst, to):
        c = copy(name, src, dst, to)
        c.start()
        started.append(c)

    def settle(keep):
        while len(started) > keep:
            started.pop(0).wait_send()

    def arrived(name, dst):
        copy(name, dst, dst, to_px).wait_recv()

    def A(zi, xi, lo=0, hi=128):
        return img.at[zi * 256 + xi * 128 + lo : zi * 256 + xi * 128 + hi, 0:CA]

    def B(zi, xi, lo=0, hi=128):
        return img.at[zi * 256 + xi * 128 + lo : zi * 256 + xi * 128 + hi, CA:1024]

    def T(s, lo=0, hi=128):
        return txt.at[s * 128 + lo : s * 128 + hi, :]

    send("T0a", T(0, 0, 64), T(1, 0, 64), to_yp)
    send("T1b", T(0, 64, 128), T(2, 64, 128), to_ym)
    send("B0", B(0, 0), B(1, 0), to_zp)
    send("B1", B(0, 0), B(2, 0), to_zm)
    send("A0", A(0, 0), A(0, 1), to_px)
    send("P0", T(0), T(4), to_next)
    def chunk(zi, xi):
        return slice(zi * 256 + xi * 128, zi * 256 + xi * 128 + 128)

    for zi, xi in mates():
        send(f"I{zi}{xi}", pairs.at[:, 0:128], pairs.at[:, chunk(SEEN[zi], xi)], at(xs[xi], zs[zi], y))
    send("T0b", T(0, 64, 128), T(1, 64, 128), to_yp)
    send("T1a", T(0, 0, 64), T(2, 0, 64), to_ym)
    send("A1", A(0, 0), A(1, 0), to_zp)
    send("A2", A(0, 0), A(2, 0), to_zm)
    send("B2", B(0, 0), B(0, 1), to_px)

    scaling = score_gain / math.sqrt(1024)
    bases = [(g * 32 + x * 16 + z * 4 + ys[s]) * 128 for s in range(4)]
    row = lax.broadcasted_iota(jnp.int32, (128, 256), 0)

    def score(slot, t):
        cols = slice(slot * 256, slot * 256 + 256)
        st = lax.dot_general(
            txt[t * 256 : t * 256 + 256, :], img[cols, :], NT, preferred_element_type=jnp.float32
        ) * scaling
        est[t * 256 : t * 256 + 256, cols] = st
        top = jnp.max(st, axis=0, keepdims=True)
        peak[:, cols] = top if t == 0 else jnp.maximum(peak[:, cols], top)

    def local_stats(slot):
        cols = slice(slot * 256, slot * 256 + 256)
        top = peak[:, cols]
        total = jnp.zeros((1, 256), jnp.float32)
        positive = jnp.zeros((1, 256), jnp.float32)
        wanted = pairs[:, cols]
        for t in range(8):
            st = est[t * 128 : t * 128 + 128, cols]
            if t < 4:
                match = row == wanted - bases[t]
                positive += jnp.sum(jnp.where(match, st, 0.0), axis=0, keepdims=True)
                chosen[t * 128 : t * 128 + 128, cols] = jnp.where(match, 1.0, 0.0).astype(jnp.bfloat16)
            e = jnp.exp(st - top)
            est[t * 128 : t * 128 + 128, cols] = e
            ebf[t * 128 : t * 128 + 128, cols] = e.astype(jnp.bfloat16)
            total += jnp.sum(e, axis=0, keepdims=True)
        stats[0, 0:1, cols] = top + jnp.log(total)
        stats[0, 1:2, cols] = positive

    arrived("B0", B(1, 0))
    send("B3", B(1, 0, 0, 64), B(3, 0, 0, 64), to_zp)
    send("B5", B(1, 0), B(1, 1), to_px)
    arrived("A0", A(0, 1))
    send("A40", A(0, 1, 0, 64), A(2, 1, 0, 64), to_zm)
    arrived("B1", B(2, 0))
    send("B4", B(2, 0, 64, 128), B(3, 0, 64, 128), to_zm)
    send("B6", B(2, 0), B(2, 1), to_px)
    send("A41", A(0, 1, 64, 128), A(2, 1, 64, 128), to_zm)
    arrived("T0a", T(1, 0, 64))
    send("P1a", T(1, 0, 64), T(5, 0, 64), to_next)
    send("T2", T(1, 0, 64), T(3, 0, 64), to_yp)
    arrived("T1b", T(2, 64, 128))
    send("P2b", T(2, 64, 128), T(6, 64, 128), to_next)
    send("T3", T(2, 64, 128), T(3, 64, 128), to_ym)
    send("A3", A(0, 1), A(1, 1), to_zp)
    arrived("T0b", T(1, 64, 128))
    send("P1b", T(1, 64, 128), T(5, 64, 128), to_next)
    arrived("T1a", T(2, 0, 64))
    send("P2a", T(2, 0, 64), T(6, 0, 64), to_next)
    arrived("A1", A(1, 0))
    send("A5", A(1, 0), A(3, 0), to_zp)
    arrived("B2", B(0, 1))
    arrived("A40", A(2, 1, 0, 64))
    send("A60", A(2, 1, 0, 64), A(3, 1, 0, 64), to_zm)
    arrived("P1a", T(5, 0, 64))
    send("U0", T(5, 0, 64), T(7, 0, 64), to_yp)
    arrived("P2b", T(6, 64, 128))
    send("U1", T(6, 64, 128), T(7, 64, 128), to_ym)
    arrived("B3", B(3, 0, 0, 64))
    arrived("B4", B(3, 0, 64, 128))
    send("B7", B(3, 0), B(3, 1), to_px)
    arrived("A41", A(2, 1, 64, 128))
    send("A61", A(2, 1, 64, 128), A(3, 1, 64, 128), to_zm)
    arrived("T2", T(3, 0, 64))
    arrived("T3", T(3, 64, 128))
    score(0, 0)
    score(0, 1)
    arrived("A3", A(1, 1))
    arrived("B5", B(1, 1))
    score(1, 0)
    score(1, 1)
    arrived("A2", A(2, 0))
    arrived("B6", B(2, 1))
    score(2, 0)
    score(2, 1)
    arrived("P0", T(4))
    arrived("P1b", T(5, 64, 128))
    score(0, 2)
    score(1, 2)
    score(2, 2)
    arrived("P2a", T(6, 0, 64))
    arrived("U0", T(7, 0, 64))
    arrived("U1", T(7, 64, 128))
    score(0, 3)
    score(1, 3)
    score(2, 3)
    for zi, xi in mates():
        arrived(f"I{SEEN[zi]}{xi}", pairs.at[:, chunk(zi, xi)])
    local_stats(0)
    local_stats(1)
    local_stats(2)
    arrived("A5", A(3, 0))
    arrived("A60", A(3, 1, 0, 64))
    arrived("A61", A(3, 1, 64, 128))
    arrived("B7", B(3, 1))
    for t in range(4):
        score(3, t)
    local_stats(3)

    for zi, xi in mates():
        send(f"S{zi}{xi}", stats.at[0], stats.at[SEEN[zi] * 2 + xi], at(xs[xi], zs[zi], y))
    def products(slot):
        rows = slice(slot * 256, slot * 256 + 256)
        gif[rows, :] = lax.dot_general(ebf[:, rows], txt[...], TN, preferred_element_type=jnp.float32)
        gis[rows, :] = lax.dot_general(chosen[:, rows], txt[0:512, :], TN, preferred_element_type=jnp.float32)

    for slot in (3, 2, 1, 0):
        products(slot)
    settle(7)
    for zi, xi in mates():
        arrived(f"S{SEEN[zi]}{xi}", stats.at[zi * 2 + xi])

    def pieces(zi, xi, r):
        out = [[None, None] for _ in range(4)]
        for i in range(4):
            for j in range(2):
                out[PLACE[zi][i]][j ^ xi] = stats[zi * 2 + xi, r : r + 1, chunk(i, j)]
        return jnp.concatenate([out[i][j] for i in range(4) for j in range(2)], axis=1)

    everyone = [(zi, xi) for zi in range(4) for xi in range(2)]
    parts = [pieces(zi, xi, 0) for zi, xi in everyone]
    top = functools.reduce(jnp.maximum, parts)
    lse = top + jnp.log(sum(jnp.exp(p - top) for p in parts))
    positive = sum(pieces(zi, xi, 1)[:, 0:128] for zi, xi in everyone)
    loss_ref[...] = (lse[:, 0:128] - positive)[0]

    factor = jnp.exp(peak[...] - lse)

    def weights(t):
        rows = slice(t * 128, t * 128 + 128)
        for slot in range(4):
            cols = slice(slot * 256, slot * 256 + 256)
            w = est[rows, cols] * factor[:, cols]
            if t < 4:
                w = jnp.where(row == pairs[:, cols] - bases[t], w - 1.0, w)
            wt[rows, cols] = w.astype(jnp.bfloat16)

    def grad_text(slot, count=1):
        rows = slice(slot * 128, (slot + count) * 128)
        gtf[rows, :] = lax.dot_general(wt[rows, :], img[...], NN, preferred_element_type=jnp.float32)

    def put(slot, lo, more=(), n=64):
        rows = slice(slot * 128 + lo, slot * 128 + lo + n)
        v = gtf[rows, :]
        for m in more:
            v = v + m.astype(jnp.float32)
        gtb[rows, :] = v.astype(jnp.bfloat16)
        return gtb.at[rows, :]

    def send_q(slot, lo, more=(), n=64):
        send(f"q{slot}{lo}", put(4 + slot, lo, more, n), rp.at[slot, lo : lo + n, :], to_last)

    def send_t(slot, lo, more=(), n=64):
        end, to = (1, to_ym) if slot == 1 else (0, to_yp)
        more = [rp[slot, lo : lo + n, :], *more]
        send(f"t{slot}{lo}", put(slot, lo, more, n), rt2.at[end, lo : lo + n, :], to)

    def gi_rows(slot, xi, lo=0, hi=128):
        return slice(slot * 256 + xi * 128 + lo, slot * 256 + xi * 128 + hi)

    def grad_image(slot):
        for k in (2 * slot, 2 * slot + 1):
            rows = slice(k * 128, k * 128 + 128)
            for c in range(8):
                cols = slice(c * 128, c * 128 + 128)
                gif[rows, cols] = gif[rows, cols] * across[rows, :] - gis[rows, cols]
        gib[gi_rows(slot, 1), CA:1024] = gif[gi_rows(slot, 1), CA:1024].astype(jnp.bfloat16)

    def send_b(slot):
        send(f"b{slot}", gib.at[gi_rows(slot, 1), CA:1024], rx.at[slot], to_px)

    def send_a(name, slot, xi, dst, to, more=(), lo=0, hi=128):
        rows = gi_rows(slot, xi, lo, hi)
        v = gif[rows, 0:CA]
        for m in more:
            v = v + m.astype(jnp.float32)
        gib[rows, 0:CA] = v.astype(jnp.bfloat16)
        send(name, gib.at[rows, 0:CA], dst, to)

    def b_sum(slot, lo, hi, more=None):
        rows = slice(slot * 256 + lo, slot * 256 + hi)
        v = gif[rows, CA:1024] + rx[slot, lo:hi, :].astype(jnp.float32)
        if more is not None:
            v = v + more.astype(jnp.float32)
        gib[rows, CA:1024] = v.astype(jnp.bfloat16)
        return gib.at[rows, CA:1024]

    weights(7)
    grad_text(7)
    for lo in (0, 32):
        send(f"u1{lo}", put(7, 64 + lo, n=32), ru.at[1, lo : lo + 32, :], to_ym)
        send(f"u0{lo}", put(7, lo, n=32), ru.at[0, lo : lo + 32, :], to_yp)
    weights(5)
    weights(6)
    grad_text(5, 2)
    send_q(1, 0)
    send_q(2, 64)
    for k in range(8):
        rows = slice(k * 128, k * 128 + 128)
        across[rows, :] = jnp.transpose(jnp.broadcast_to(factor[:, rows], (128, 128)))
    grad_image(3)
    send_a("a1", 3, 1, ra1.at[1], to_zm)
    send_a("a0", 3, 0, ra1.at[0], to_zp)
    send_b(3)
    for t in range(5):
        weights(t)
    grad_text(3, 2)
    send("t0", put(3, 0), rt1.at[0], to_yp)
    send("t1", put(3, 64), rt1.at[1], to_ym)
    grad_image(2)
    send_b(2)
    send_a("a3", 2, 1, ra2.at[0, 1], to_zp)
    grad_image(1)
    send_a("a2", 1, 0, ra2.at[1, 0], to_zm)
    send_b(1)
    for lo in (0, 32):
        arrived(f"u1{lo}", ru.at[1, lo : lo + 32, :])
        send_q(1, 64 + lo, [ru[1, lo : lo + 32, :]], 32)
        arrived(f"u0{lo}", ru.at[0, lo : lo + 32, :])
        send_q(2, lo, [ru[0, lo : lo + 32, :]], 32)
    send_q(0, 0)
    send_q(0, 64)
    grad_image(0)
    send_b(0)
    arrived("a1", ra1.at[1])
    for half in range(2):
        lo = half * 64
        send_a(
            f"a5{half}", 1, 1, ra2.at[1, 1, lo : lo + 64, :], to_zm, [ra1[1, lo : lo + 64, :]], lo, lo + 64
        )
        if half == 0:
            arrived("b3", rx.at[3])
            send("b5", b_sum(3, 64, 128), rb1.at[1], to_zm)
            send("b4", b_sum(3, 0, 64), rb1.at[0], to_zp)
    arrived("a0", ra1.at[0])
    send_a("a4", 2, 0, ra2.at[0, 0], to_zp, [ra1[0]])
    grad_text(1, 2)
    arrived("q10", rp.at[1, 0:64, :])
    send_t(1, 0)
    arrived("q264", rp.at[2, 64:128, :])
    send_t(2, 64)
    grad_text(0)
    arrived("t1", rt1.at[1])
    arrived("q164", rp.at[1, 64:96, :])
    send_t(1, 64, [rt1[1, 0:32, :]], 32)
    arrived("t0", rt1.at[0])
    arrived("q20", rp.at[2, 0:32, :])
    send_t(2, 0, [rt1[0, 0:32, :]], 32)
    arrived("b2", rx.at[2])
    b_sum(2, 64, 128)
    arrived("q196", rp.at[1, 96:128, :])
    send_t(1, 96, [rt1[1, 32:64, :]], 32)
    arrived("q232", rp.at[2, 32:64, :])
    send_t(2, 32, [rt1[0, 32:64, :]], 32)
    arrived("a3", ra2.at[0, 1])
    arrived("a50", ra2.at[1, 1, 0:64, :])
    send_a("a60", 0, 1, ra3.at[0:64, :], to_px, [ra2[0, 1, 0:64, :], ra2[1, 1, 0:64, :]], 0, 64)
    arrived("b4", rb1.at[0])
    b_sum(2, 0, 64, rb1[0])
    send("b7", gib.at[gi_rows(2, 0), CA:1024], rb2.at[0], to_zp)
    settle(14)
    arrived("b1", rx.at[1])
    b_sum(1, 0, 64)
    arrived("b5", rb1.at[1])
    b_sum(1, 64, 128, rb1[1])
    send("b6", gib.at[gi_rows(1, 0), CA:1024], rb2.at[1], to_zm)
    arrived("a51", ra2.at[1, 1, 64:128, :])
    send_a("a61", 0, 1, ra3.at[64:128, :], to_px, [ra2[0, 1, 64:128, :], ra2[1, 1, 64:128, :]], 64, 128)

    settle(5)
    for lo in (0, 64):
        arrived(f"q0{lo}", rp.at[0, lo : lo + 64, :])
    for lo, n in ((0, 64), (64, 32), (96, 32)):
        arrived(f"t1{lo}", rt2.at[1, lo : lo + n, :])
    for lo, n in ((0, 32), (32, 32), (64, 64)):
        arrived(f"t2{lo}", rt2.at[0, lo : lo + n, :])
    gt_ref[...] = (
        gtf[0:128, :] + rp[0].astype(jnp.float32) + rt2[0].astype(jnp.float32)
    )
    gt_last_ref[...] = rt2[1]
    arrived("b0", rx.at[0])
    arrived("b6", rb2.at[1])
    arrived("b7", rb2.at[0])
    gi_ref[:, CA:1024] = (
        gif[0:128, CA:1024] + rx[0].astype(jnp.float32) + rb2[0].astype(jnp.float32)
    )
    gi_last_ref[:, CA:1024] = rb2[1]
    arrived("a2", ra2.at[1, 0])
    arrived("a4", ra2.at[0, 0])
    arrived("a60", ra3.at[0:64, :])
    arrived("a61", ra3.at[64:128, :])
    gi_ref[:, 0:CA] = (
        gif[0:128, 0:CA] + ra2[0, 0].astype(jnp.float32) + ra2[1, 0].astype(jnp.float32)
    )
    gi_last_ref[:, 0:CA] = ra3[...]
    assert len(names) <= 112
    settle(0)


def local(image, text, pair):
    bf16, f32 = jnp.bfloat16, jnp.float32
    vmem = pl.BlockSpec(memory_space=pltpu.VMEM)
    hbm = pl.BlockSpec(memory_space=pltpu.HBM)
    CB = 1024 - CA
    loss, grad_image, grad_text, image_last, text_last = pl.pallas_call(
        kernel,
        out_shape=(
            jax.ShapeDtypeStruct((128,), f32),
            jax.ShapeDtypeStruct((128, 1024), f32),
            jax.ShapeDtypeStruct((128, 1024), f32),
            jax.ShapeDtypeStruct((128, 1024), bf16),
            jax.ShapeDtypeStruct((128, 1024), bf16),
        ),
        in_specs=[hbm, hbm, vmem],
        out_specs=(vmem,) * 5,
        scratch_shapes=[
            pltpu.VMEM((1024, 1024), bf16),
            pltpu.VMEM((1024, 1024), bf16),
            pltpu.VMEM((1, 1024), jnp.int32),
            pltpu.VMEM((1024, 1024), f32),
            pltpu.VMEM((1, 1024), f32),
            pltpu.VMEM((8, 2, 1024), f32),
            pltpu.VMEM((1024, 1024), bf16),
            pltpu.VMEM((1024, 1024), bf16),
            pltpu.VMEM((512, 1024), bf16),
            pltpu.VMEM((1024, 128), f32),
            pltpu.VMEM((1024, 1024), f32),
            pltpu.VMEM((1024, 1024), f32),
            pltpu.VMEM((1024, 1024), bf16),
            pltpu.VMEM((1024, 1024), f32),
            pltpu.VMEM((1024, 1024), bf16),
            pltpu.VMEM((2, 64, 1024), bf16),
            pltpu.VMEM((3, 128, 1024), bf16),
            pltpu.VMEM((4, 128, CB), bf16),
            pltpu.VMEM((2, 128, CA), bf16),
            pltpu.VMEM((2, 2, 128, CA), bf16),
            pltpu.VMEM((128, CA), bf16),
            pltpu.VMEM((2, 64, CB), bf16),
            pltpu.VMEM((2, 128, CB), bf16),
            pltpu.VMEM((2, 64, 1024), bf16),
            pltpu.VMEM((2, 128, 1024), bf16),
            pltpu.SemaphoreType.DMA((112,)),
            pltpu.SemaphoreType.DMA((112,)),
            pltpu.SemaphoreType.DMA((2,)),
        ],
        compiler_params=pltpu.CompilerParams(
            collective_id=0, has_side_effects=True, vmem_limit_bytes=52 * 1024 * 1024 + 128 * 1024
        ),
        cost_estimate=pl.CostEstimate(
            flops=6 * 1024**3, bytes_accessed=2 * 1024 * 1024, transcendentals=1024 * 1024
        ),
    )(image, text, pair.reshape(1, 128))
    return loss, grad_image + image_last.astype(f32), grad_text + text_last.astype(f32)


def solution(mesh):
    in_specs = (P(("group", "blk"), None), P(("group", "blk"), None), P(("group", "blk")))
    out_specs = (P(("group", "blk")), P(("group", "blk"), None), P(("group", "blk"), None))
    return jax.shard_map(local, mesh=mesh, in_specs=in_specs, out_specs=out_specs, check_vma=False)
```

```python
import functools
import math

import jax
import jax.numpy as jnp
from jax import lax
from jax.experimental import pallas as pl
from jax.experimental.pallas import tpu as pltpu
from jax.sharding import PartitionSpec as P

MESH = pl.DeviceIdType.MESH
score_gain = 2.5
CA = 512
NT = (((1,), (1,)), ((), ()))
TN = (((0,), (0,)), ((), ()))
NN = (((1,), (0,)), ((), ()))

OFFSET = (0, 3, 1, 2)
PLACE = [[OFFSET.index((OFFSET[a] + OFFSET[i]) % 4) for i in range(4)] for a in range(4)]
SEEN = [OFFSET.index((4 - OFFSET[a]) % 4) for a in range(4)]


def kernel(
    image_ref, text_ref, pair_ref, loss_ref, gi_ref, gt_ref, gi_last_ref, gt_last_ref,
    img, txt, pairs, est, peak, stats, wt,
    ebf, chosen, across, gis, gif, gib, gtf, gtb, ru, rp, rx, ra1, ra2, ra3, rb1, rb2, rt1, rt2,
    send_sem, recv_sem, local_sem,
):
    g = lax.axis_index("group")
    b = lax.axis_index("blk")
    x, z, y = b // 16, (b // 4) % 4, b % 4
    px = 1 - x
    zs = [(z + o) % 4 for o in OFFSET]
    ys = [(y + o) % 4 for o in OFFSET]
    xs = [x, px]

    def at(xx, zz, yy):
        return (g, xx * 16 + zz * 4 + yy)

    def mates():
        return [(zi, xi) for zi in range(4) for xi in range(2) if (zi, xi) != (0, 0)]

    to_px = at(px, z, y)
    to_zm, to_zp = at(x, zs[1], y), at(x, zs[2], y)
    to_ym, to_yp = at(x, z, ys[1]), at(x, z, ys[2])
    next_g, last_g = (g + 1) % 4, (g + 3) % 4
    flip = lambda even: jnp.where(even, px, x)
    to_next = (next_g, flip(next_g % 2 == 0) * 16 + z * 4 + y)
    to_last = (last_g, flip(g % 2 == 0) * 16 + z * 4 + y)

    barrier = pltpu.get_barrier_semaphore()
    peers = [at(xs[xi], zs[zi], y) for zi, xi in mates()] + [to_ym, to_yp, to_next, to_last]
    for peer in peers:
        pl.semaphore_signal(barrier, inc=1, device_id=peer, device_id_type=MESH)

    text_in = pltpu.make_async_copy(text_ref, gtf.at[0:128, :], local_sem.at[0])
    image_in = pltpu.make_async_copy(image_ref, gif.at[0:128, :], local_sem.at[1])
    text_in.start()
    image_in.start()
    pairs[:, 0:128] = pair_ref[...]
    text_in.wait()
    txt[0:128, :] = gtf[0:128, :].astype(jnp.bfloat16)
    image_in.wait()
    img[0:128, :] = gif[0:128, :].astype(jnp.bfloat16)

    pl.semaphore_wait(barrier, len(peers))

    names = {}
    started = []

    def copy(name, src, dst, to):
        k = names.setdefault(name, len(names))
        return pltpu.make_async_remote_copy(
            src_ref=src, dst_ref=dst, send_sem=send_sem.at[k], recv_sem=recv_sem.at[k],
            device_id=to, device_id_type=MESH,
        )

    def send(name, src, dst, to):
        c = copy(name, src, dst, to)
        c.start()
        started.append(c)

    def settle(keep):
        while len(started) > keep:
            started.pop(0).wait_send()

    def arrived(name, dst):
        copy(name, dst, dst, to_px).wait_recv()

    def A(zi, xi, lo=0, hi=128):
        return img.at[zi * 256 + xi * 128 + lo : zi * 256 + xi * 128 + hi, 0:CA]

    def B(zi, xi, lo=0, hi=128):
        return img.at[zi * 256 + xi * 128 + lo : zi * 256 + xi * 128 + hi, CA:1024]

    def T(s, lo=0, hi=128):
        return txt.at[s * 128 + lo : s * 128 + hi, :]

    send("T0a", T(0, 0, 64), T(1, 0, 64), to_yp)
    send("T1b", T(0, 64, 128), T(2, 64, 128), to_ym)
    send("B0", B(0, 0), B(1, 0), to_zp)
    send("B1", B(0, 0), B(2, 0), to_zm)
    send("A0", A(0, 0), A(0, 1), to_px)
    send("P0", T(0), T(4), to_next)
    def chunk(zi, xi):
        return slice(zi * 256 + xi * 128, zi * 256 + xi * 128 + 128)

    for zi, xi in mates():
        send(f"I{zi}{xi}", pairs.at[:, 0:128], pairs.at[:, chunk(SEEN[zi], xi)], at(xs[xi], zs[zi], y))
    send("T0b", T(0, 64, 128), T(1, 64, 128), to_yp)
    send("T1a", T(0, 0, 64), T(2, 0, 64), to_ym)
    send("A1", A(0, 0), A(1, 0), to_zp)
    send("A2", A(0, 0), A(2, 0), to_zm)
    send("B2", B(0, 0), B(0, 1), to_px)

    scaling = score_gain / math.sqrt(1024)
    bases = [(g * 32 + x * 16 + z * 4 + ys[s]) * 128 for s in range(4)]
    row = lax.broadcasted_iota(jnp.int32, (128, 256), 0)

    def score(slot, t):
        cols = slice(slot * 256, slot * 256 + 256)
        st = lax.dot_general(
            txt[t * 256 : t * 256 + 256, :], img[cols, :], NT, preferred_element_type=jnp.float32
        ) * scaling
        est[t * 256 : t * 256 + 256, cols] = st
        top = jnp.max(st, axis=0, keepdims=True)
        peak[:, cols] = top if t == 0 else jnp.maximum(peak[:, cols], top)

    def local_stats(slot):
        cols = slice(slot * 256, slot * 256 + 256)
        top = peak[:, cols]
        total = jnp.zeros((1, 256), jnp.float32)
        positive = jnp.zeros((1, 256), jnp.float32)
        wanted = pairs[:, cols]
        for t in range(8):
            st = est[t * 128 : t * 128 + 128, cols]
            if t < 4:
                match = row == wanted - bases[t]
                positive += jnp.sum(jnp.where(match, st, 0.0), axis=0, keepdims=True)
                chosen[t * 128 : t * 128 + 128, cols] = jnp.where(match, 1.0, 0.0).astype(jnp.bfloat16)
            e = jnp.exp(st - top)
            est[t * 128 : t * 128 + 128, cols] = e
            ebf[t * 128 : t * 128 + 128, cols] = e.astype(jnp.bfloat16)
            total += jnp.sum(e, axis=0, keepdims=True)
        stats[0, 0:1, cols] = top + jnp.log(total)
        stats[0, 1:2, cols] = positive

    arrived("B0", B(1, 0))
    send("B3", B(1, 0, 0, 64), B(3, 0, 0, 64), to_zp)
    send("B5", B(1, 0), B(1, 1), to_px)
    arrived("A0", A(0, 1))
    send("A40", A(0, 1, 0, 64), A(2, 1, 0, 64), to_zm)
    arrived("B1", B(2, 0))
    send("B4", B(2, 0, 64, 128), B(3, 0, 64, 128), to_zm)
    send("B6", B(2, 0), B(2, 1), to_px)
    send("A41", A(0, 1, 64, 128), A(2, 1, 64, 128), to_zm)
    arrived("T0a", T(1, 0, 64))
    send("P1a", T(1, 0, 64), T(5, 0, 64), to_next)
    send("T2", T(1, 0, 64), T(3, 0, 64), to_yp)
    arrived("T1b", T(2, 64, 128))
    send("P2b", T(2, 64, 128), T(6, 64, 128), to_next)
    send("T3", T(2, 64, 128), T(3, 64, 128), to_ym)
    send("A3", A(0, 1), A(1, 1), to_zp)
    arrived("T0b", T(1, 64, 128))
    send("P1b", T(1, 64, 128), T(5, 64, 128), to_next)
    arrived("T1a", T(2, 0, 64))
    send("P2a", T(2, 0, 64), T(6, 0, 64), to_next)
    arrived("A1", A(1, 0))
    send("A5", A(1, 0), A(3, 0), to_zp)
    arrived("B2", B(0, 1))
    arrived("A40", A(2, 1, 0, 64))
    send("A60", A(2, 1, 0, 64), A(3, 1, 0, 64), to_zm)
    arrived("P1a", T(5, 0, 64))
    send("U0", T(5, 0, 64), T(7, 0, 64), to_yp)
    arrived("P2b", T(6, 64, 128))
    send("U1", T(6, 64, 128), T(7, 64, 128), to_ym)
    arrived("B3", B(3, 0, 0, 64))
    arrived("B4", B(3, 0, 64, 128))
    send("B7", B(3, 0), B(3, 1), to_px)
    arrived("A41", A(2, 1, 64, 128))
    send("A61", A(2, 1, 64, 128), A(3, 1, 64, 128), to_zm)
    arrived("T2", T(3, 0, 64))
    arrived("T3", T(3, 64, 128))
    score(0, 0)
    score(0, 1)
    arrived("A3", A(1, 1))
    arrived("B5", B(1, 1))
    score(1, 0)
    score(1, 1)
    arrived("A2", A(2, 0))
    arrived("B6", B(2, 1))
    score(2, 0)
    score(2, 1)
    arrived("P0", T(4))
    arrived("P1b", T(5, 64, 128))
    score(0, 2)
    score(1, 2)
    score(2, 2)
    arrived("P2a", T(6, 0, 64))
    arrived("U0", T(7, 0, 64))
    arrived("U1", T(7, 64, 128))
    score(0, 3)
    score(1, 3)
    score(2, 3)
    for zi, xi in mates():
        arrived(f"I{SEEN[zi]}{xi}", pairs.at[:, chunk(zi, xi)])
    local_stats(0)
    local_stats(1)
    local_stats(2)
    arrived("A5", A(3, 0))
    arrived("A60", A(3, 1, 0, 64))
    arrived("A61", A(3, 1, 64, 128))
    arrived("B7", B(3, 1))
    for t in range(4):
        score(3, t)
    local_stats(3)

    for zi, xi in mates():
        send(f"S{zi}{xi}", stats.at[0], stats.at[SEEN[zi] * 2 + xi], at(xs[xi], zs[zi], y))
    def products(slot):
        rows = slice(slot * 256, slot * 256 + 256)
        gif[rows, :] = lax.dot_general(ebf[:, rows], txt[...], TN, preferred_element_type=jnp.float32)
        gis[rows, :] = lax.dot_general(chosen[:, rows], txt[0:512, :], TN, preferred_element_type=jnp.float32)

    for slot in (3, 2, 1, 0):
        products(slot)
    settle(7)
    for zi, xi in mates():
        arrived(f"S{SEEN[zi]}{xi}", stats.at[zi * 2 + xi])

    def pieces(zi, xi, r):
        out = [[None, None] for _ in range(4)]
        for i in range(4):
            for j in range(2):
                out[PLACE[zi][i]][j ^ xi] = stats[zi * 2 + xi, r : r + 1, chunk(i, j)]
        return jnp.concatenate([out[i][j] for i in range(4) for j in range(2)], axis=1)

    everyone = [(zi, xi) for zi in range(4) for xi in range(2)]
    parts = [pieces(zi, xi, 0) for zi, xi in everyone]
    top = functools.reduce(jnp.maximum, parts)
    lse = top + jnp.log(sum(jnp.exp(p - top) for p in parts))
    positive = sum(pieces(zi, xi, 1)[:, 0:128] for zi, xi in everyone)
    loss_ref[...] = (lse[:, 0:128] - positive)[0]

    factor = jnp.exp(peak[...] - lse)

    def weights(t):
        rows = slice(t * 128, t * 128 + 128)
        for slot in range(4):
            cols = slice(slot * 256, slot * 256 + 256)
            w = est[rows, cols] * factor[:, cols]
            if t < 4:
                w = jnp.where(row == pairs[:, cols] - bases[t], w - 1.0, w)
            wt[rows, cols] = w.astype(jnp.bfloat16)

    def grad_text(slot, count=1):
        rows = slice(slot * 128, (slot + count) * 128)
        gtf[rows, :] = lax.dot_general(wt[rows, :], img[...], NN, preferred_element_type=jnp.float32)

    def put(slot, lo, more=(), n=64):
        rows = slice(slot * 128 + lo, slot * 128 + lo + n)
        v = gtf[rows, :]
        for m in more:
            v = v + m.astype(jnp.float32)
        gtb[rows, :] = v.astype(jnp.bfloat16)
        return gtb.at[rows, :]

    def send_q(slot, lo, more=(), n=64):
        send(f"q{slot}{lo}", put(4 + slot, lo, more, n), rp.at[slot, lo : lo + n, :], to_last)

    def send_t(slot, lo, more=(), n=64):
        end, to = (1, to_ym) if slot == 1 else (0, to_yp)
        more = [rp[slot, lo : lo + n, :], *more]
        send(f"t{slot}{lo}", put(slot, lo, more, n), rt2.at[end, lo : lo + n, :], to)

    def gi_rows(slot, xi, lo=0, hi=128):
        return slice(slot * 256 + xi * 128 + lo, slot * 256 + xi * 128 + hi)

    def grad_image(slot):
        for k in (2 * slot, 2 * slot + 1):
            rows = slice(k * 128, k * 128 + 128)
            for c in range(8):
                cols = slice(c * 128, c * 128 + 128)
                gif[rows, cols] = gif[rows, cols] * across[rows, :] - gis[rows, cols]
        gib[gi_rows(slot, 1), CA:1024] = gif[gi_rows(slot, 1), CA:1024].astype(jnp.bfloat16)

    def send_b(slot):
        send(f"b{slot}", gib.at[gi_rows(slot, 1), CA:1024], rx.at[slot], to_px)

    def send_a(name, slot, xi, dst, to, more=(), lo=0, hi=128):
        rows = gi_rows(slot, xi, lo, hi)
        v = gif[rows, 0:CA]
        for m in more:
            v = v + m.astype(jnp.float32)
        gib[rows, 0:CA] = v.astype(jnp.bfloat16)
        send(name, gib.at[rows, 0:CA], dst, to)

    def b_sum(slot, lo, hi, more=None):
        rows = slice(slot * 256 + lo, slot * 256 + hi)
        v = gif[rows, CA:1024] + rx[slot, lo:hi, :].astype(jnp.float32)
        if more is not None:
            v = v + more.astype(jnp.float32)
        gib[rows, CA:1024] = v.astype(jnp.bfloat16)
        return gib.at[rows, CA:1024]

    weights(7)
    grad_text(7)
    for lo in (0, 32):
        send(f"u1{lo}", put(7, 64 + lo, n=32), ru.at[1, lo : lo + 32, :], to_ym)
        send(f"u0{lo}", put(7, lo, n=32), ru.at[0, lo : lo + 32, :], to_yp)
    weights(5)
    weights(6)
    grad_text(5, 2)
    send_q(1, 0)
    send_q(2, 64)
    for k in range(8):
        rows = slice(k * 128, k * 128 + 128)
        across[rows, :] = jnp.transpose(jnp.broadcast_to(factor[:, rows], (128, 128)))
    grad_image(3)
    send_a("a1", 3, 1, ra1.at[1], to_zm)
    send_a("a0", 3, 0, ra1.at[0], to_zp)
    send_b(3)
    for t in range(5):
        weights(t)
    grad_text(3, 2)
    send("t0", put(3, 0), rt1.at[0], to_yp)
    send("t1", put(3, 64), rt1.at[1], to_ym)
    grad_image(2)
    send_b(2)
    send_a("a3", 2, 1, ra2.at[0, 1], to_zp)
    grad_image(1)
    send_a("a2", 1, 0, ra2.at[1, 0], to_zm)
    send_b(1)
    for lo in (0, 32):
        arrived(f"u1{lo}", ru.at[1, lo : lo + 32, :])
        send_q(1, 64 + lo, [ru[1, lo : lo + 32, :]], 32)
        arrived(f"u0{lo}", ru.at[0, lo : lo + 32, :])
        send_q(2, lo, [ru[0, lo : lo + 32, :]], 32)
    send_q(0, 0)
    send_q(0, 64)
    grad_image(0)
    send_b(0)
    arrived("a1", ra1.at[1])
    for half in range(2):
        lo = half * 64
        send_a(
            f"a5{half}", 1, 1, ra2.at[1, 1, lo : lo + 64, :], to_zm, [ra1[1, lo : lo + 64, :]], lo, lo + 64
        )
        if half == 0:
            arrived("b3", rx.at[3])
            send("b5", b_sum(3, 64, 128), rb1.at[1], to_zm)
            send("b4", b_sum(3, 0, 64), rb1.at[0], to_zp)
    arrived("a0", ra1.at[0])
    send_a("a4", 2, 0, ra2.at[0, 0], to_zp, [ra1[0]])
    grad_text(1, 2)
    arrived("q10", rp.at[1, 0:64, :])
    send_t(1, 0)
    arrived("q264", rp.at[2, 64:128, :])
    send_t(2, 64)
    grad_text(0)
    arrived("t1", rt1.at[1])
    arrived("q164", rp.at[1, 64:96, :])
    send_t(1, 64, [rt1[1, 0:32, :]], 32)
    arrived("t0", rt1.at[0])
    arrived("q20", rp.at[2, 0:32, :])
    send_t(2, 0, [rt1[0, 0:32, :]], 32)
    arrived("b2", rx.at[2])
    b_sum(2, 64, 128)
    arrived("q196", rp.at[1, 96:128, :])
    send_t(1, 96, [rt1[1, 32:64, :]], 32)
    arrived("q232", rp.at[2, 32:64, :])
    send_t(2, 32, [rt1[0, 32:64, :]], 32)
    arrived("a3", ra2.at[0, 1])
    arrived("a50", ra2.at[1, 1, 0:64, :])
    send_a("a60", 0, 1, ra3.at[0:64, :], to_px, [ra2[0, 1, 0:64, :], ra2[1, 1, 0:64, :]], 0, 64)
    arrived("b4", rb1.at[0])
    b_sum(2, 0, 64, rb1[0])
    send("b7", gib.at[gi_rows(2, 0), CA:1024], rb2.at[0], to_zp)
    settle(14)
    arrived("b1", rx.at[1])
    b_sum(1, 0, 64)
    arrived("b5", rb1.at[1])
    b_sum(1, 64, 128, rb1[1])
    send("b6", gib.at[gi_rows(1, 0), CA:1024], rb2.at[1], to_zm)
    arrived("a51", ra2.at[1, 1, 64:128, :])
    send_a("a61", 0, 1, ra3.at[64:128, :], to_px, [ra2[0, 1, 64:128, :], ra2[1, 1, 64:128, :]], 64, 128)

    settle(5)
    arrived("b0", rx.at[0])
    arrived("b7", rb2.at[0])
    gi_ref[:, CA:1024] = (
        gif[0:128, CA:1024] + rx[0].astype(jnp.float32) + rb2[0].astype(jnp.float32)
    )
    arrived("a2", ra2.at[1, 0])
    arrived("a4", ra2.at[0, 0])
    gi_ref[:, 0:CA] = (
        gif[0:128, 0:CA] + ra2[0, 0].astype(jnp.float32) + ra2[1, 0].astype(jnp.float32)
    )
    for lo in (0, 64):
        arrived(f"q0{lo}", rp.at[0, lo : lo + 64, :])
    for lo, n in ((64, 64), (0, 32), (32, 32)):
        arrived(f"t2{lo}", rt2.at[0, lo : lo + n, :])
    gt_ref[...] = (
        gtf[0:128, :] + rp[0].astype(jnp.float32) + rt2[0].astype(jnp.float32)
    )
    for lo, n in ((0, 64), (64, 32), (96, 32)):
        arrived(f"t1{lo}", rt2.at[1, lo : lo + n, :])
    gt_last_ref[...] = rt2[1]
    arrived("b6", rb2.at[1])
    gi_last_ref[:, CA:1024] = rb2[1]
    arrived("a60", ra3.at[0:64, :])
    arrived("a61", ra3.at[64:128, :])
    gi_last_ref[:, 0:CA] = ra3[...]
    assert len(names) <= 112
    settle(0)


def local(image, text, pair):
    bf16, f32 = jnp.bfloat16, jnp.float32
    vmem = pl.BlockSpec(memory_space=pltpu.VMEM)
    hbm = pl.BlockSpec(memory_space=pltpu.HBM)
    CB = 1024 - CA
    loss, grad_image, grad_text, image_last, text_last = pl.pallas_call(
        kernel,
        out_shape=(
            jax.ShapeDtypeStruct((128,), f32),
            jax.ShapeDtypeStruct((128, 1024), f32),
            jax.ShapeDtypeStruct((128, 1024), f32),
            jax.ShapeDtypeStruct((128, 1024), bf16),
            jax.ShapeDtypeStruct((128, 1024), bf16),
        ),
        in_specs=[hbm, hbm, vmem],
        out_specs=(vmem,) * 5,
        scratch_shapes=[
            pltpu.VMEM((1024, 1024), bf16),
            pltpu.VMEM((1024, 1024), bf16),
            pltpu.VMEM((1, 1024), jnp.int32),
            pltpu.VMEM((1024, 1024), f32),
            pltpu.VMEM((1, 1024), f32),
            pltpu.VMEM((8, 2, 1024), f32),
            pltpu.VMEM((1024, 1024), bf16),
            pltpu.VMEM((1024, 1024), bf16),
            pltpu.VMEM((512, 1024), bf16),
            pltpu.VMEM((1024, 128), f32),
            pltpu.VMEM((1024, 1024), f32),
            pltpu.VMEM((1024, 1024), f32),
            pltpu.VMEM((1024, 1024), bf16),
            pltpu.VMEM((1024, 1024), f32),
            pltpu.VMEM((1024, 1024), bf16),
            pltpu.VMEM((2, 64, 1024), bf16),
            pltpu.VMEM((3, 128, 1024), bf16),
            pltpu.VMEM((4, 128, CB), bf16),
            pltpu.VMEM((2, 128, CA), bf16),
            pltpu.VMEM((2, 2, 128, CA), bf16),
            pltpu.VMEM((128, CA), bf16),
            pltpu.VMEM((2, 64, CB), bf16),
            pltpu.VMEM((2, 128, CB), bf16),
            pltpu.VMEM((2, 64, 1024), bf16),
            pltpu.VMEM((2, 128, 1024), bf16),
            pltpu.SemaphoreType.DMA((112,)),
            pltpu.SemaphoreType.DMA((112,)),
            pltpu.SemaphoreType.DMA((2,)),
        ],
        compiler_params=pltpu.CompilerParams(
            collective_id=0, has_side_effects=True, vmem_limit_bytes=52 * 1024 * 1024 + 128 * 1024
        ),
        cost_estimate=pl.CostEstimate(
            flops=6 * 1024**3, bytes_accessed=2 * 1024 * 1024, transcendentals=1024 * 1024
        ),
    )(image, text, pair.reshape(1, 128))
    return loss, grad_image + image_last.astype(f32), grad_text + text_last.astype(f32)


def solution(mesh):
    in_specs = (P(("group", "blk"), None), P(("group", "blk"), None), P(("group", "blk")))
    out_specs = (P(("group", "blk")), P(("group", "blk"), None), P(("group", "blk"), None))
    return jax.shard_map(local, mesh=mesh, in_specs=in_specs, out_specs=out_specs, check_vma=False)
```

```python
import functools
import math

import jax
import jax.numpy as jnp
from jax import lax
from jax.experimental import pallas as pl
from jax.experimental.pallas import tpu as pltpu
from jax.sharding import PartitionSpec as P

MESH = pl.DeviceIdType.MESH
score_gain = 2.5
CA = 512
NT = (((1,), (1,)), ((), ()))
TN = (((0,), (0,)), ((), ()))
NN = (((1,), (0,)), ((), ()))

OFFSET = (0, 3, 1, 2)
PLACE = [[OFFSET.index((OFFSET[a] + OFFSET[i]) % 4) for i in range(4)] for a in range(4)]
SEEN = [OFFSET.index((4 - OFFSET[a]) % 4) for a in range(4)]


def kernel(
    image_ref, text_ref, pair_ref, loss_ref, gi_ref, gt_ref, gi_last_ref, gt_last_ref,
    img, txt, pairs, est, peak, stats, wt,
    ebf, chosen, across, gis, gif, gib, gtf, gtb, ru, rp, rx, ra1, ra2, ra3, rb1, rb2, rt1, rt2,
    send_sem, recv_sem, local_sem,
):
    g = lax.axis_index("group")
    b = lax.axis_index("blk")
    x, z, y = b // 16, (b // 4) % 4, b % 4
    px = 1 - x
    zs = [(z + o) % 4 for o in OFFSET]
    ys = [(y + o) % 4 for o in OFFSET]
    xs = [x, px]

    def at(xx, zz, yy):
        return (g, xx * 16 + zz * 4 + yy)

    def mates():
        return [(zi, xi) for zi in range(4) for xi in range(2) if (zi, xi) != (0, 0)]

    to_px = at(px, z, y)
    to_zm, to_zp = at(x, zs[1], y), at(x, zs[2], y)
    to_ym, to_yp = at(x, z, ys[1]), at(x, z, ys[2])
    next_g, last_g = (g + 1) % 4, (g + 3) % 4
    flip = lambda even: jnp.where(even, px, x)
    to_next = (next_g, flip(next_g % 2 == 0) * 16 + z * 4 + y)
    to_last = (last_g, flip(g % 2 == 0) * 16 + z * 4 + y)

    barrier = pltpu.get_barrier_semaphore()
    peers = [at(xs[xi], zs[zi], y) for zi, xi in mates()] + [to_ym, to_yp, to_next, to_last]
    for peer in peers:
        pl.semaphore_signal(barrier, inc=1, device_id=peer, device_id_type=MESH)

    text_in = pltpu.make_async_copy(text_ref, gtf.at[0:128, :], local_sem.at[0])
    image_in = pltpu.make_async_copy(image_ref, gif.at[0:128, :], local_sem.at[1])
    text_in.start()
    image_in.start()
    pairs[:, 0:128] = pair_ref[...]
    text_in.wait()
    txt[0:128, :] = gtf[0:128, :].astype(jnp.bfloat16)

    pl.semaphore_wait(barrier, len(peers))

    names = {}
    started = []

    def copy(name, src, dst, to):
        k = names.setdefault(name, len(names))
        return pltpu.make_async_remote_copy(
            src_ref=src, dst_ref=dst, send_sem=send_sem.at[k], recv_sem=recv_sem.at[k],
            device_id=to, device_id_type=MESH,
        )

    def send(name, src, dst, to):
        c = copy(name, src, dst, to)
        c.start()
        started.append(c)

    def settle(keep):
        while len(started) > keep:
            started.pop(0).wait_send()

    def arrived(name, dst):
        copy(name, dst, dst, to_px).wait_recv()

    def A(zi, xi, lo=0, hi=128):
        return img.at[zi * 256 + xi * 128 + lo : zi * 256 + xi * 128 + hi, 0:CA]

    def B(zi, xi, lo=0, hi=128):
        return img.at[zi * 256 + xi * 128 + lo : zi * 256 + xi * 128 + hi, CA:1024]

    def T(s, lo=0, hi=128):
        return txt.at[s * 128 + lo : s * 128 + hi, :]

    send("T0a", T(0, 0, 64), T(1, 0, 64), to_yp)
    send("T1b", T(0, 64, 128), T(2, 64, 128), to_ym)
    send("P0", T(0), T(4), to_next)
    image_in.wait()
    img[0:128, :] = gif[0:128, :].astype(jnp.bfloat16)
    send("B0", B(0, 0), B(1, 0), to_zp)
    send("B1", B(0, 0), B(2, 0), to_zm)
    send("A0", A(0, 0), A(0, 1), to_px)
    def chunk(zi, xi):
        return slice(zi * 256 + xi * 128, zi * 256 + xi * 128 + 128)

    for zi, xi in mates():
        send(f"I{zi}{xi}", pairs.at[:, 0:128], pairs.at[:, chunk(SEEN[zi], xi)], at(xs[xi], zs[zi], y))
    send("T0b", T(0, 64, 128), T(1, 64, 128), to_yp)
    send("T1a", T(0, 0, 64), T(2, 0, 64), to_ym)
    send("A1", A(0, 0), A(1, 0), to_zp)
    send("A2", A(0, 0), A(2, 0), to_zm)
    send("B2", B(0, 0), B(0, 1), to_px)

    scaling = score_gain / math.sqrt(1024)
    bases = [(g * 32 + x * 16 + z * 4 + ys[s]) * 128 for s in range(4)]
    row = lax.broadcasted_iota(jnp.int32, (128, 256), 0)

    def score(slot, t):
        cols = slice(slot * 256, slot * 256 + 256)
        st = lax.dot_general(
            txt[t * 256 : t * 256 + 256, :], img[cols, :], NT, preferred_element_type=jnp.float32
        ) * scaling
        est[t * 256 : t * 256 + 256, cols] = st
        top = jnp.max(st, axis=0, keepdims=True)
        peak[:, cols] = top if t == 0 else jnp.maximum(peak[:, cols], top)

    def local_stats(slot):
        cols = slice(slot * 256, slot * 256 + 256)
        top = peak[:, cols]
        total = jnp.zeros((1, 256), jnp.float32)
        positive = jnp.zeros((1, 256), jnp.float32)
        wanted = pairs[:, cols]
        for t in range(8):
            st = est[t * 128 : t * 128 + 128, cols]
            if t < 4:
                match = row == wanted - bases[t]
                positive += jnp.sum(jnp.where(match, st, 0.0), axis=0, keepdims=True)
                chosen[t * 128 : t * 128 + 128, cols] = jnp.where(match, 1.0, 0.0).astype(jnp.bfloat16)
            e = jnp.exp(st - top)
            est[t * 128 : t * 128 + 128, cols] = e
            ebf[t * 128 : t * 128 + 128, cols] = e.astype(jnp.bfloat16)
            total += jnp.sum(e, axis=0, keepdims=True)
        stats[0, 0:1, cols] = top + jnp.log(total)
        stats[0, 1:2, cols] = positive

    arrived("B0", B(1, 0))
    send("B3", B(1, 0, 0, 64), B(3, 0, 0, 64), to_zp)
    send("B5", B(1, 0), B(1, 1), to_px)
    arrived("A0", A(0, 1))
    send("A40", A(0, 1, 0, 64), A(2, 1, 0, 64), to_zm)
    arrived("B1", B(2, 0))
    send("B4", B(2, 0, 64, 128), B(3, 0, 64, 128), to_zm)
    send("B6", B(2, 0), B(2, 1), to_px)
    send("A41", A(0, 1, 64, 128), A(2, 1, 64, 128), to_zm)
    arrived("T0a", T(1, 0, 64))
    send("P1a", T(1, 0, 64), T(5, 0, 64), to_next)
    send("T2", T(1, 0, 64), T(3, 0, 64), to_yp)
    arrived("T1b", T(2, 64, 128))
    send("P2b", T(2, 64, 128), T(6, 64, 128), to_next)
    send("T3", T(2, 64, 128), T(3, 64, 128), to_ym)
    send("A3", A(0, 1), A(1, 1), to_zp)
    arrived("T0b", T(1, 64, 128))
    send("P1b", T(1, 64, 128), T(5, 64, 128), to_next)
    arrived("T1a", T(2, 0, 64))
    send("P2a", T(2, 0, 64), T(6, 0, 64), to_next)
    arrived("A1", A(1, 0))
    send("A5", A(1, 0), A(3, 0), to_zp)
    arrived("B2", B(0, 1))
    arrived("A40", A(2, 1, 0, 64))
    send("A60", A(2, 1, 0, 64), A(3, 1, 0, 64), to_zm)
    arrived("P1a", T(5, 0, 64))
    send("U0", T(5, 0, 64), T(7, 0, 64), to_yp)
    arrived("P2b", T(6, 64, 128))
    send("U1", T(6, 64, 128), T(7, 64, 128), to_ym)
    arrived("B3", B(3, 0, 0, 64))
    arrived("B4", B(3, 0, 64, 128))
    send("B7", B(3, 0), B(3, 1), to_px)
    arrived("A41", A(2, 1, 64, 128))
    send("A61", A(2, 1, 64, 128), A(3, 1, 64, 128), to_zm)
    arrived("T2", T(3, 0, 64))
    arrived("T3", T(3, 64, 128))
    score(0, 0)
    score(0, 1)
    arrived("A3", A(1, 1))
    arrived("B5", B(1, 1))
    score(1, 0)
    score(1, 1)
    arrived("A2", A(2, 0))
    arrived("B6", B(2, 1))
    score(2, 0)
    score(2, 1)
    arrived("P0", T(4))
    arrived("P1b", T(5, 64, 128))
    score(0, 2)
    score(1, 2)
    score(2, 2)
    arrived("P2a", T(6, 0, 64))
    arrived("U0", T(7, 0, 64))
    arrived("U1", T(7, 64, 128))
    score(0, 3)
    score(1, 3)
    score(2, 3)
    for zi, xi in mates():
        arrived(f"I{SEEN[zi]}{xi}", pairs.at[:, chunk(zi, xi)])
    local_stats(0)
    local_stats(1)
    local_stats(2)
    arrived("A5", A(3, 0))
    arrived("A60", A(3, 1, 0, 64))
    arrived("A61", A(3, 1, 64, 128))
    arrived("B7", B(3, 1))
    for t in range(4):
        score(3, t)
    local_stats(3)

    for zi, xi in mates():
        send(f"S{zi}{xi}", stats.at[0], stats.at[SEEN[zi] * 2 + xi], at(xs[xi], zs[zi], y))
    def products(slot):
        rows = slice(slot * 256, slot * 256 + 256)
        gif[rows, :] = lax.dot_general(ebf[:, rows], txt[...], TN, preferred_element_type=jnp.float32)
        gis[rows, :] = lax.dot_general(chosen[:, rows], txt[0:512, :], TN, preferred_element_type=jnp.float32)

    for slot in (3, 2, 1, 0):
        products(slot)
    settle(7)
    for zi, xi in mates():
        arrived(f"S{SEEN[zi]}{xi}", stats.at[zi * 2 + xi])

    def pieces(zi, xi, r):
        out = [[None, None] for _ in range(4)]
        for i in range(4):
            for j in range(2):
                out[PLACE[zi][i]][j ^ xi] = stats[zi * 2 + xi, r : r + 1, chunk(i, j)]
        return jnp.concatenate([out[i][j] for i in range(4) for j in range(2)], axis=1)

    everyone = [(zi, xi) for zi in range(4) for xi in range(2)]
    parts = [pieces(zi, xi, 0) for zi, xi in everyone]
    top = functools.reduce(jnp.maximum, parts)
    lse = top + jnp.log(sum(jnp.exp(p - top) for p in parts))
    positive = sum(pieces(zi, xi, 1)[:, 0:128] for zi, xi in everyone)
    loss_ref[...] = (lse[:, 0:128] - positive)[0]

    factor = jnp.exp(peak[...] - lse)

    def weights(t):
        rows = slice(t * 128, t * 128 + 128)
        for slot in range(4):
            cols = slice(slot * 256, slot * 256 + 256)
            w = est[rows, cols] * factor[:, cols]
            if t < 4:
                w = jnp.where(row == pairs[:, cols] - bases[t], w - 1.0, w)
            wt[rows, cols] = w.astype(jnp.bfloat16)

    def grad_text(slot, count=1):
        rows = slice(slot * 128, (slot + count) * 128)
        gtf[rows, :] = lax.dot_general(wt[rows, :], img[...], NN, preferred_element_type=jnp.float32)

    def put(slot, lo, more=(), n=64):
        rows = slice(slot * 128 + lo, slot * 128 + lo + n)
        v = gtf[rows, :]
        for m in more:
            v = v + m.astype(jnp.float32)
        gtb[rows, :] = v.astype(jnp.bfloat16)
        return gtb.at[rows, :]

    def send_q(slot, lo, more=(), n=64):
        send(f"q{slot}{lo}", put(4 + slot, lo, more, n), rp.at[slot, lo : lo + n, :], to_last)

    def send_t(slot, lo, more=(), n=64):
        end, to = (1, to_ym) if slot == 1 else (0, to_yp)
        more = [rp[slot, lo : lo + n, :], *more]
        send(f"t{slot}{lo}", put(slot, lo, more, n), rt2.at[end, lo : lo + n, :], to)

    def gi_rows(slot, xi, lo=0, hi=128):
        return slice(slot * 256 + xi * 128 + lo, slot * 256 + xi * 128 + hi)

    def grad_image(slot):
        for k in (2 * slot, 2 * slot + 1):
            rows = slice(k * 128, k * 128 + 128)
            for c in range(8):
                cols = slice(c * 128, c * 128 + 128)
                gif[rows, cols] = gif[rows, cols] * across[rows, :] - gis[rows, cols]
        gib[gi_rows(slot, 1), CA:1024] = gif[gi_rows(slot, 1), CA:1024].astype(jnp.bfloat16)

    def send_b(slot):
        send(f"b{slot}", gib.at[gi_rows(slot, 1), CA:1024], rx.at[slot], to_px)

    def send_a(name, slot, xi, dst, to, more=(), lo=0, hi=128):
        rows = gi_rows(slot, xi, lo, hi)
        v = gif[rows, 0:CA]
        for m in more:
            v = v + m.astype(jnp.float32)
        gib[rows, 0:CA] = v.astype(jnp.bfloat16)
        send(name, gib.at[rows, 0:CA], dst, to)

    def b_sum(slot, lo, hi, more=None):
        rows = slice(slot * 256 + lo, slot * 256 + hi)
        v = gif[rows, CA:1024] + rx[slot, lo:hi, :].astype(jnp.float32)
        if more is not None:
            v = v + more.astype(jnp.float32)
        gib[rows, CA:1024] = v.astype(jnp.bfloat16)
        return gib.at[rows, CA:1024]

    weights(7)
    grad_text(7)
    for lo in (0, 32):
        send(f"u1{lo}", put(7, 64 + lo, n=32), ru.at[1, lo : lo + 32, :], to_ym)
        send(f"u0{lo}", put(7, lo, n=32), ru.at[0, lo : lo + 32, :], to_yp)
    weights(5)
    weights(6)
    grad_text(5, 2)
    send_q(1, 0)
    send_q(2, 64)
    for k in range(8):
        rows = slice(k * 128, k * 128 + 128)
        across[rows, :] = jnp.transpose(jnp.broadcast_to(factor[:, rows], (128, 128)))
    grad_image(3)
    send_a("a1", 3, 1, ra1.at[1], to_zm)
    send_a("a0", 3, 0, ra1.at[0], to_zp)
    send_b(3)
    for t in range(5):
        weights(t)
    grad_text(3, 2)
    send("t0", put(3, 0), rt1.at[0], to_yp)
    send("t1", put(3, 64), rt1.at[1], to_ym)
    grad_image(2)
    send_b(2)
    send_a("a3", 2, 1, ra2.at[0, 1], to_zp)
    grad_image(1)
    send_a("a2", 1, 0, ra2.at[1, 0], to_zm)
    send_b(1)
    for lo in (0, 32):
        arrived(f"u1{lo}", ru.at[1, lo : lo + 32, :])
        send_q(1, 64 + lo, [ru[1, lo : lo + 32, :]], 32)
        arrived(f"u0{lo}", ru.at[0, lo : lo + 32, :])
        send_q(2, lo, [ru[0, lo : lo + 32, :]], 32)
    send_q(0, 0)
    send_q(0, 64)
    grad_image(0)
    send_b(0)
    arrived("a1", ra1.at[1])
    for half in range(2):
        lo = half * 64
        send_a(
            f"a5{half}", 1, 1, ra2.at[1, 1, lo : lo + 64, :], to_zm, [ra1[1, lo : lo + 64, :]], lo, lo + 64
        )
        if half == 0:
            arrived("b3", rx.at[3])
            send("b5", b_sum(3, 64, 128), rb1.at[1], to_zm)
            send("b4", b_sum(3, 0, 64), rb1.at[0], to_zp)
    arrived("a0", ra1.at[0])
    send_a("a4", 2, 0, ra2.at[0, 0], to_zp, [ra1[0]])
    grad_text(1, 2)
    arrived("q10", rp.at[1, 0:64, :])
    send_t(1, 0)
    arrived("q264", rp.at[2, 64:128, :])
    send_t(2, 64)
    grad_text(0)
    arrived("t1", rt1.at[1])
    arrived("q164", rp.at[1, 64:96, :])
    send_t(1, 64, [rt1[1, 0:32, :]], 32)
    arrived("t0", rt1.at[0])
    arrived("q20", rp.at[2, 0:32, :])
    send_t(2, 0, [rt1[0, 0:32, :]], 32)
    arrived("b2", rx.at[2])
    b_sum(2, 64, 128)
    arrived("q196", rp.at[1, 96:128, :])
    send_t(1, 96, [rt1[1, 32:64, :]], 32)
    arrived("q232", rp.at[2, 32:64, :])
    send_t(2, 32, [rt1[0, 32:64, :]], 32)
    arrived("a3", ra2.at[0, 1])
    arrived("a50", ra2.at[1, 1, 0:64, :])
    send_a("a60", 0, 1, ra3.at[0:64, :], to_px, [ra2[0, 1, 0:64, :], ra2[1, 1, 0:64, :]], 0, 64)
    arrived("b4", rb1.at[0])
    b_sum(2, 0, 64, rb1[0])
    send("b7", gib.at[gi_rows(2, 0), CA:1024], rb2.at[0], to_zp)
    settle(14)
    arrived("b1", rx.at[1])
    b_sum(1, 0, 64)
    arrived("b5", rb1.at[1])
    b_sum(1, 64, 128, rb1[1])
    send("b6", gib.at[gi_rows(1, 0), CA:1024], rb2.at[1], to_zm)
    arrived("a51", ra2.at[1, 1, 64:128, :])
    send_a("a61", 0, 1, ra3.at[64:128, :], to_px, [ra2[0, 1, 64:128, :], ra2[1, 1, 64:128, :]], 64, 128)

    settle(5)
    arrived("b0", rx.at[0])
    arrived("b7", rb2.at[0])
    gi_ref[:, CA:1024] = (
        gif[0:128, CA:1024] + rx[0].astype(jnp.float32) + rb2[0].astype(jnp.float32)
    )
    arrived("a2", ra2.at[1, 0])
    arrived("a4", ra2.at[0, 0])
    gi_ref[:, 0:CA] = (
        gif[0:128, 0:CA] + ra2[0, 0].astype(jnp.float32) + ra2[1, 0].astype(jnp.float32)
    )
    for lo in (0, 64):
        arrived(f"q0{lo}", rp.at[0, lo : lo + 64, :])
    for lo, n in ((64, 64), (0, 32), (32, 32)):
        arrived(f"t2{lo}", rt2.at[0, lo : lo + n, :])
    gt_ref[...] = (
        gtf[0:128, :] + rp[0].astype(jnp.float32) + rt2[0].astype(jnp.float32)
    )
    for lo, n in ((0, 64), (64, 32), (96, 32)):
        arrived(f"t1{lo}", rt2.at[1, lo : lo + n, :])
    gt_last_ref[...] = rt2[1]
    arrived("b6", rb2.at[1])
    gi_last_ref[:, CA:1024] = rb2[1]
    arrived("a60", ra3.at[0:64, :])
    arrived("a61", ra3.at[64:128, :])
    gi_last_ref[:, 0:CA] = ra3[...]
    assert len(names) <= 112
    settle(0)


def local(image, text, pair):
    bf16, f32 = jnp.bfloat16, jnp.float32
    vmem = pl.BlockSpec(memory_space=pltpu.VMEM)
    hbm = pl.BlockSpec(memory_space=pltpu.HBM)
    CB = 1024 - CA
    loss, grad_image, grad_text, image_last, text_last = pl.pallas_call(
        kernel,
        out_shape=(
            jax.ShapeDtypeStruct((128,), f32),
            jax.ShapeDtypeStruct((128, 1024), f32),
            jax.ShapeDtypeStruct((128, 1024), f32),
            jax.ShapeDtypeStruct((128, 1024), bf16),
            jax.ShapeDtypeStruct((128, 1024), bf16),
        ),
        in_specs=[hbm, hbm, vmem],
        out_specs=(vmem,) * 5,
        scratch_shapes=[
            pltpu.VMEM((1024, 1024), bf16),
            pltpu.VMEM((1024, 1024), bf16),
            pltpu.VMEM((1, 1024), jnp.int32),
            pltpu.VMEM((1024, 1024), f32),
            pltpu.VMEM((1, 1024), f32),
            pltpu.VMEM((8, 2, 1024), f32),
            pltpu.VMEM((1024, 1024), bf16),
            pltpu.VMEM((1024, 1024), bf16),
            pltpu.VMEM((512, 1024), bf16),
            pltpu.VMEM((1024, 128), f32),
            pltpu.VMEM((1024, 1024), f32),
            pltpu.VMEM((1024, 1024), f32),
            pltpu.VMEM((1024, 1024), bf16),
            pltpu.VMEM((1024, 1024), f32),
            pltpu.VMEM((1024, 1024), bf16),
            pltpu.VMEM((2, 64, 1024), bf16),
            pltpu.VMEM((3, 128, 1024), bf16),
            pltpu.VMEM((4, 128, CB), bf16),
            pltpu.VMEM((2, 128, CA), bf16),
            pltpu.VMEM((2, 2, 128, CA), bf16),
            pltpu.VMEM((128, CA), bf16),
            pltpu.VMEM((2, 64, CB), bf16),
            pltpu.VMEM((2, 128, CB), bf16),
            pltpu.VMEM((2, 64, 1024), bf16),
            pltpu.VMEM((2, 128, 1024), bf16),
            pltpu.SemaphoreType.DMA((112,)),
            pltpu.SemaphoreType.DMA((112,)),
            pltpu.SemaphoreType.DMA((2,)),
        ],
        compiler_params=pltpu.CompilerParams(
            collective_id=0, has_side_effects=True, vmem_limit_bytes=52 * 1024 * 1024 + 128 * 1024
        ),
        cost_estimate=pl.CostEstimate(
            flops=6 * 1024**3, bytes_accessed=2 * 1024 * 1024, transcendentals=1024 * 1024
        ),
    )(image, text, pair.reshape(1, 128))
    return loss, grad_image + image_last.astype(f32), grad_text + text_last.astype(f32)


def solution(mesh):
    in_specs = (P(("group", "blk"), None), P(("group", "blk"), None), P(("group", "blk")))
    out_specs = (P(("group", "blk")), P(("group", "blk"), None), P(("group", "blk"), None))
    return jax.shard_map(local, mesh=mesh, in_specs=in_specs, out_specs=out_specs, check_vma=False)
```
